512 devices in a mesh: blk: 32 (over y, z_lo), wide: 16 (over z_hi, x, core).
Axes of the slice: x: 4, y: 4, z: 16 (z_hi: 2, z_lo: 8; z = z_hi * 8 + z_lo), core: 2. Of those that a mesh axis runs over, the one named last changes fastest.
Arguments:
- source_latent: bfloat16 [65536, 64], P('blk'), may hold values from -2.5 to 2.5
- source_logw: float32 [65536], P('blk'), may hold values from -1.5 to 1.5
- target_latent: bfloat16 [131072, 64], P(('wide', 'blk')), may hold values from -3 to 3
- target_logw: float32 [131072], P(('wide', 'blk')), may hold values from -1.5 to 5
- target_potential: float32 [131072], P(('wide', 'blk')), may hold values from -3 to 90
Outputs:
- source_potential: float32 [65536], P('blk')
- new_target_potential: float32 [131072], P(('wide', 'blk'))
The draws below stay inside these ranges and needn't reach their ends.
All inputs are finite; a program needn't handle non-finite values.
Results may differ from the reference program's by a relative error of at most 0.0003.
Values may be sent and summed in bfloat16 or wider, within the bound.
No kernel may reach another device: no remote copies, remote signals or barrier semaphores. Data moves between devices by JAX's collectives and lax.ppermute only.
A program may use at most 64 MiB of HBM per device.

```python
import math
import jax
import jax.numpy as jnp
from jax import lax

D = 64
NS = 65536
NT = 131072


def draw_target_latent(key, part):
    key = jax.random.fold_in(key, 11)
    values = jnp.clip(0.3 * jax.random.normal(key, (NT, D), jnp.float32), -1.5, 1.5)
    return values.astype(jnp.bfloat16)


def draw_target_potential(key, part):
    key = jax.random.fold_in(key, 12)
    values = jnp.clip(0.5 * jax.random.normal(key, (NT,), jnp.float32), -2.5, 2.5)
    return values


def draw_target_logw(key, part):
    key = jax.random.fold_in(key, 13)
    fraction = jnp.arange(NT).astype(jnp.float32) / NT
    values = jax.random.uniform(key, (NT,), jnp.float32, -1.5, 1.5) + math.log(10.0) * fraction
    return values


def block_scale(own_key, extent, cuts, least, high):
    def one(position, shards_of):
        heights = jax.random.uniform(jax.random.fold_in(jax.random.fold_in(own_key, 6), position), (shards_of,), jnp.float32, least / len(cuts), high / len(cuts))
        return jnp.repeat(jnp.exp(heights), extent[position] // shards_of).reshape((-1,) + (1,) * (len(extent) - position - 1))

    level = one(*cuts[0])
    for cut in cuts[1:]:
        level = level * one(*cut)
    return level


def centred(stream_key, dims, scale, reach, shards=(), held_as=jnp.bfloat16):
    drawn = jax.random.normal(stream_key, dims, jnp.float32) * scale
    if len(shards) > 0:
        drawn = block_scale(stream_key, dims, shards, -0.22, 0.18) * drawn
    return jnp.clip(drawn, min=-reach, max=reach).astype(held_as)


def setup_inputs(seed: int = 0) -> dict:
    arg_keys = jax.random.split(jax.random.key(seed), 6)
    return {
        "source_latent": centred(arg_keys[0], (NS, D), 0.3, 2.5, ((0, 32),)),
        "source_logw": jnp.clip(jax.random.uniform(arg_keys[1], (NS,), jnp.float32, -1.5, 1.5) * block_scale(arg_keys[1], (NS,), ((0, 32),), -0.4, 0.0), -1.5, 1.5),
        "target_latent": draw_target_latent(jax.random.fold_in(arg_keys[5], 71), 0),
        "target_logw": draw_target_logw(jax.random.fold_in(arg_keys[5], 71), 0),
        "target_potential": draw_target_potential(jax.random.fold_in(arg_keys[5], 71), 0),
    }


epsilon = 0.5


def combine(first, second):
    highest = jnp.maximum(first[0], second[0])
    return (highest, first[1] * jnp.exp(first[0] - highest) + second[1] * jnp.exp(second[0] - highest))


def partial_lse(row_latent, row_squares, col_latent, col_squares, col_offset):
    rows, width = row_latent.shape
    cols = col_latent.shape[0]
    row_block = math.gcd(rows, 2048)
    col_block = math.gcd(cols, 2048)
    col_parts = (col_latent.reshape(cols // col_block, col_block, width),
                 col_squares.reshape(cols // col_block, col_block),
                 col_offset.reshape(cols // col_block, col_block))

    def one_rows(inputs):
        latent, squares = inputs

        def advance(running, portion):
            clatent, csquares, coffset = portion
            inner = jnp.dot(latent, clatent.T, preferred_element_type=jnp.float32)
            cost = 0.5 * (squares[:, None] + csquares[None, :]) - inner
            score = coffset[None, :] - cost / epsilon
            highest = jnp.max(score, axis=1)
            masses = jnp.sum(jnp.exp(score - highest[:, None]), axis=1)
            return combine(running, (highest, masses)), None

        initial = (jnp.full((row_block,), -1e30, jnp.float32), jnp.zeros((row_block,), jnp.float32))
        result, unused = lax.scan(advance, initial, col_parts)
        return result

    maxima, masses = lax.map(one_rows, (row_latent.reshape(rows // row_block, row_block, width),
                                        row_squares.reshape(rows // row_block, row_block)))
    return maxima.reshape(rows), masses.reshape(rows)


def reference(source_latent, source_logw, target_latent, target_logw, target_potential):
    source_sq = jnp.sum(jnp.square(source_latent.astype(jnp.float32)), axis=1)
    target_sq = jnp.sum(jnp.square(target_latent.astype(jnp.float32)), axis=1)
    target_offset = target_potential / epsilon + target_logw
    maxima, masses = partial_lse(source_latent, source_sq, target_latent, target_sq, target_offset)
    source_potential = -epsilon * (maxima + jnp.log(masses))
    source_offset = source_potential / epsilon + source_logw
    maxima, masses = partial_lse(target_latent, target_sq, source_latent, source_sq, source_offset)
    new_target_potential = -epsilon * (maxima + jnp.log(masses))
    return (source_potential, new_target_potential)
```

```python
import functools

import jax
import jax.numpy as jnp
from jax import lax
from jax.experimental import pallas as pl
from jax.experimental.pallas import tpu as pltpu
from jax.sharding import PartitionSpec as P

ZRUN = 8
FEATURES = 64
EXTRA = 16
DEPTH = 128
LANES = 1024
STEP = 256
LOW = 2.0**-60
HIGH = 2.0**120


def three_parts(value):
    high = value.astype(jnp.bfloat16).astype(jnp.float32)
    rest = value - high
    middle = rest.astype(jnp.bfloat16).astype(jnp.float32)
    low = (rest - middle).astype(jnp.bfloat16).astype(jnp.float32)
    return high, middle, low


def extra_block(first, second):
    n = first[0].shape[1]
    row = lax.broadcasted_iota(jnp.int32, (EXTRA, n), 0)
    block = jnp.zeros((EXTRA, n), jnp.float32)
    for k, part in enumerate(tuple(first) + tuple(second)):
        block = jnp.where(row == k, part, block)
    return block


def ones_of(n):
    one = jnp.ones((1, n), jnp.float32)
    return one, one, one


def prepare_kernel(y_ref, logw_ref, potential_ref, out_ref, offset_ref):
    y = y_ref[...].astype(jnp.float32)
    offset = potential_ref[...] * 2.0 + logw_ref[...]
    bias = offset - jnp.sum(y * y, axis=0, keepdims=True)
    out_ref[0:FEATURES, :] = (y * 2.0).astype(jnp.bfloat16)
    out_ref[FEATURES : FEATURES + EXTRA, :] = extra_block(
        three_parts(bias), ones_of(bias.shape[1])
    ).astype(jnp.bfloat16)
    offset_ref[...] = offset


def lay_sources(x_refs, xs_ref):
    per = x_refs[0].shape[1]
    for r, x_ref in enumerate(x_refs):
        xs_ref[0:FEATURES, r * per : (r + 1) * per] = x_ref[...]


def weights_at(xs_ref, at):
    part = xs_ref[:, at]
    rest = jnp.zeros((DEPTH - part.shape[0], part.shape[1]), part.dtype)
    return jnp.concatenate([part, rest], axis=0)


def product(a, b):
    return jnp.dot(a, b, preferred_element_type=jnp.float32)


def folded(value, combine):
    rows, n = value.shape
    return combine(value.reshape(rows // 8, 8, n), axis=0)


def join(a, b):
    top = jnp.maximum(a, b)
    return top + jnp.log(1.0 + jnp.exp(jnp.minimum(a, b) - top))


def first_kernel(ny, last, *refs):
    y_ref, x_refs, refs = refs[0], refs[1 : 1 + ny], refs[1 + ny :]
    if last:
        place_ref, before_ref, logw_ref, refs = refs[0], refs[1], refs[2], refs[3:]
    yt_ref, l_ref, xs_ref, sums_ref = refs
    rows = yt_ref.shape[0]
    per = x_refs[0].shape[1]
    cols = ny * per
    wide = min(LANES, cols)
    row_step = min(STEP, rows)
    col_step = min(STEP, wide)

    extra = y_ref[FEATURES : FEATURES + EXTRA, :].astype(jnp.float32)
    bias = extra[0:1, :] + extra[1:2, :] + extra[2:3, :]
    shift = jnp.max(bias, axis=1, keepdims=True)
    for k in range(0, rows, row_step):
        block = jnp.concatenate(
            [
                y_ref[:, k : k + row_step].astype(jnp.float32),
                jnp.zeros((DEPTH - FEATURES - EXTRA, row_step), jnp.float32),
            ],
            axis=0,
        )
        yt_ref[k : k + row_step, :] = block.T.astype(jnp.bfloat16)
    lay_sources(x_refs, xs_ref)
    xs_ref[FEATURES : FEATURES + EXTRA, :] = extra_block(
        ones_of(cols), three_parts(jnp.broadcast_to(-shift, (1, cols)))
    ).astype(jnp.bfloat16)

    def store(row, value):
        if last:
            here = pl.ds(place_ref[0] ^ row, 1)
            l_ref[here, :] = join(before_ref[row : row + 1, :], value)
        else:
            l_ref[row : row + 1, :] = value

    if last:
        l_ref[...] = jnp.zeros(l_ref.shape, jnp.float32)
        l_ref[pl.ds(ny + place_ref[0], 1), :] = logw_ref[...]

    def main(g, carry):
        for t in range(wide // col_step):
            at = pl.ds(pl.multiple_of(g * wide + t * col_step, col_step), col_step)
            weights = weights_at(xs_ref, at)
            total = jnp.zeros((8, col_step), jnp.float32)
            for j in range(rows // row_step):
                score = product(yt_ref[j * row_step : (j + 1) * row_step, :], weights)
                total = total + folded(jnp.exp(score), jnp.sum)
            sums_ref[:, at] = total
        return carry

    lax.fori_loop(0, cols // wide, main, 0)
    total = jnp.sum(sums_ref[...], axis=0, keepdims=True)
    result = shift + jnp.log(total)
    for r in range(ny):
        store(r, result[:, r * per : (r + 1) * per])

    @pl.when(jnp.logical_not((jnp.min(total) > LOW) & (jnp.max(total) < HIGH)))
    def _():
        def again(g, carry):
            at = pl.ds(pl.multiple_of(g * col_step, col_step), col_step)
            weights = weights_at(xs_ref, at)

            def advance(j, state):
                top, total = state
                here = pl.ds(pl.multiple_of(j * row_step, row_step), row_step)
                score = product(yt_ref[here, :], weights)
                new = jnp.maximum(top, jnp.max(score, axis=0, keepdims=True))
                total = total * jnp.exp(top - new) + jnp.sum(
                    jnp.exp(score - new), axis=0, keepdims=True
                )
                return new, total

            start = (
                jnp.full((1, col_step), -1e30, jnp.float32),
                jnp.zeros((1, col_step), jnp.float32),
            )
            top, total = lax.fori_loop(0, rows // row_step, advance, start)
            sums_ref[0:1, at] = shift + top + jnp.log(total)
            return carry

        lax.fori_loop(0, cols // col_step, again, 0)
        for r in range(ny):
            store(r, sums_ref[0:1, r * per : (r + 1) * per])


def second_kernel(ny, *refs):
    yt_ref, x_refs, place_ref, c_ref = refs[0], refs[1 : 1 + ny], refs[1 + ny], refs[2 + ny]
    s_ref, xs_ref, acc_ref, top_ref = refs[3 + ny :]
    rows = yt_ref.shape[0]
    nz, each = s_ref.shape
    per = x_refs[0].shape[1]
    cols = ny * per
    row_step = min(STEP, rows)
    col_step = min(STEP, cols)

    lay_sources(x_refs, xs_ref)
    for r in range(ny):
        c = c_ref[pl.ds(place_ref[0] ^ r, 1), :]
        xs_ref[FEATURES : FEATURES + EXTRA, r * per : (r + 1) * per] = extra_block(
            ones_of(per), three_parts(c)
        ).astype(jnp.bfloat16)

    def lanes_folded(value, combine):
        out = value[:, 0:128]
        for k in range(1, value.shape[1] // 128):
            out = combine(out, value[:, k * 128 : (k + 1) * 128])
        return out

    def main(g, carry):
        here = pl.ds(pl.multiple_of(g * row_step, row_step), row_step)
        left = yt_ref[here, :]
        total = jnp.zeros((row_step, 128), jnp.float32)
        for t in range(cols // col_step):
            score = product(left, weights_at(xs_ref, slice(t * col_step, (t + 1) * col_step)))
            total = total + lanes_folded(jnp.exp(score), jnp.add)
        acc_ref[here, :] = total
        return carry

    lax.fori_loop(0, rows // row_step, main, 0)
    total = jnp.sum(acc_ref[...].T, axis=0, keepdims=True)
    result = jnp.log(total)
    for k in range(nz):
        s_ref[k : k + 1, :] = result[:, k * each : (k + 1) * each]

    @pl.when(jnp.logical_not((jnp.min(total) > LOW) & (jnp.max(total) < HIGH)))
    def _():
        def again(g, carry):
            here = pl.ds(pl.multiple_of(g * row_step, row_step), row_step)
            left = yt_ref[here, :]

            def advance(t, state):
                top, total = state
                at = pl.ds(pl.multiple_of(t * col_step, col_step), col_step)
                score = product(left, weights_at(xs_ref, at))
                new = jnp.maximum(top, lanes_folded(score, jnp.maximum))
                total = total * jnp.exp(top - new)
                for k in range(col_step // 128):
                    total = total + jnp.exp(score[:, k * 128 : (k + 1) * 128] - new)
                return new, total

            start = (
                jnp.full((row_step, 128), -1e30, jnp.float32),
                jnp.zeros((row_step, 128), jnp.float32),
            )
            top, total = lax.fori_loop(0, cols // col_step, advance, start)
            top_ref[here, :] = top
            acc_ref[here, :] = total
            return carry

        lax.fori_loop(0, rows // row_step, again, 0)
        tops = top_ref[...].T
        top = jnp.max(tops, axis=0, keepdims=True)
        total = jnp.sum(acc_ref[...].T * jnp.exp(tops - top), axis=0, keepdims=True)
        result = top + jnp.log(total)
        for k in range(nz):
            s_ref[k : k + 1, :] = result[:, k * each : (k + 1) * each]


def call(kernel, outs, scratch, flops, exps, *args, scalars=()):
    return pl.pallas_call(
        kernel,
        out_shape=outs,
        in_specs=[
            pl.BlockSpec(memory_space=pltpu.SMEM if k in scalars else pltpu.VMEM)
            for k in range(len(args))
        ],
        scratch_shapes=scratch,
        compiler_params=pltpu.CompilerParams(vmem_limit_bytes=40 * 2**20),
        cost_estimate=pl.CostEstimate(
            flops=flops, bytes_accessed=4 * 2**20, transcendentals=exps
        ),
    )(*args)


def per_device(nz, ny, nw, source_latent, source_logw, target_latent, target_logw, target_potential):
    f32, bf16 = jnp.float32, jnp.bfloat16
    per = source_latent.shape[0]
    each = target_latent.shape[0]
    cols, half = ny * per, nz // 2 * each
    pairs = cols * half
    place = lax.axis_index("blk") // nz
    place_in = place.astype(jnp.int32).reshape(1)
    depth = FEATURES + EXTRA

    def along_y(value, r):
        perm = [(y * nz + z, (y ^ r) * nz + z) for y in range(ny) for z in range(nz)]
        return lax.ppermute(value, "blk", perm)

    def along_z(value, k):
        perm = [(y * nz + z, y * nz + (z ^ k)) for y in range(ny) for z in range(nz)]
        return lax.ppermute(value, "blk", perm)

    def along_wide(value, k):
        return lax.ppermute(value, "wide", [(w, w ^ k) for w in range(nw)])

    y, offset = call(
        prepare_kernel,
        (jax.ShapeDtypeStruct((depth, each), bf16), jax.ShapeDtypeStruct((1, each), f32)),
        [],
        each * FEATURES * 4,
        0,
        target_latent.T,
        target_logw.reshape(1, each),
        target_potential.reshape(1, each),
    )
    x = source_latent.T
    xs = [x] + [along_y(x, r) for r in range(1, ny)]
    bit = nz // 2
    while bit > 1:
        y = jnp.concatenate([y, along_z(y, bit)], axis=1)
        bit //= 2
    *xs, y = lax.optimization_barrier((*xs, y))
    far = along_z(y, 1)

    def first(block, *more):
        last = len(more) > 0
        return call(
            functools.partial(first_kernel, ny, last),
            (
                jax.ShapeDtypeStruct((half, DEPTH), bf16),
                jax.ShapeDtypeStruct((2 * ny if last else ny, per), f32),
            ),
            [pltpu.VMEM((depth, cols), bf16), pltpu.VMEM((8, cols), f32)],
            2 * pairs * DEPTH,
            pairs,
            block,
            *xs,
            *more,
            scalars=(1 + ny,),
        )

    yt_near, total = first(y)
    yt_far, total = first(far, place_in, total, source_logw.reshape(1, per))
    bit = 1
    while bit < ny:
        other = along_y(total, bit)
        row = lax.broadcasted_iota(jnp.int32, total.shape, 0)
        total = jnp.where(row < ny, join(total, other), total + other)
        bit *= 2
    total, logw = total[:ny], total[ny:]
    bit = 1
    while bit < nw:
        total = join(total, along_wide(total, bit))
        bit *= 2
    c = logw - total
    sq = jnp.sum(jnp.square(x.astype(f32)), axis=0, keepdims=True)
    mine = lax.dynamic_slice(total, (place, 0), (1, per))
    source_potential = -0.5 * (mine - sq)

    def second(block):
        return call(
            functools.partial(second_kernel, ny),
            jax.ShapeDtypeStruct((nz // 2, each), f32),
            [
                pltpu.VMEM((depth, cols), bf16),
                pltpu.VMEM((half, 128), f32),
                pltpu.VMEM((half, 128), f32),
            ],
            2 * pairs * DEPTH,
            pairs,
            block,
            *xs,
            place_in,
            c,
            scalars=(1 + ny,),
        )

    away = second(yt_far)
    yt_near, away = lax.optimization_barrier((yt_near, away))
    other = along_z(away, 1)
    sums = join(second(yt_near), other)
    bit = 2
    while bit < nz:
        count = sums.shape[0] // 2
        sums = join(sums[:count], along_z(sums[count:], bit))
        bit *= 2
    new_target_potential = -0.5 * (sums - offset)
    return source_potential.reshape(per), new_target_potential.reshape(each)


def solution(mesh):
    nz = ZRUN
    ny = mesh.shape["blk"] // nz
    nw = mesh.shape["wide"]
    placed = (
        P("blk", None),
        P("blk"),
        P(("wide", "blk"), None),
        P(("wide", "blk")),
        P(("wide", "blk")),
    )
    return jax.shard_map(
        functools.partial(per_device, nz, ny, nw),
        mesh=mesh,
        in_specs=placed,
        out_specs=(P("blk"), P(("wide", "blk"))),
        check_vma=False,
    )
```

```python
import functools

import jax
import jax.numpy as jnp
from jax import lax
from jax.experimental import pallas as pl
from jax.experimental.pallas import tpu as pltpu
from jax.sharding import PartitionSpec as P

ZRUN = 8
FEATURES = 64
EXTRA = 16
DEPTH = 128
LANES = 1024
STEP = 256
LOW = 2.0**-60
HIGH = 2.0**120


def three_parts(value):
    high = value.astype(jnp.bfloat16).astype(jnp.float32)
    rest = value - high
    middle = rest.astype(jnp.bfloat16).astype(jnp.float32)
    low = (rest - middle).astype(jnp.bfloat16).astype(jnp.float32)
    return high, middle, low


def extra_block(first, second):
    n = first[0].shape[1]
    row = lax.broadcasted_iota(jnp.int32, (EXTRA, n), 0)
    block = jnp.zeros((EXTRA, n), jnp.float32)
    for k, part in enumerate(tuple(first) + tuple(second)):
        block = jnp.where(row == k, part, block)
    return block


def ones_of(n):
    one = jnp.ones((1, n), jnp.float32)
    return one, one, one


def prepare_kernel(y_ref, logw_ref, potential_ref, out_ref, offset_ref):
    y = y_ref[...].astype(jnp.float32)
    offset = potential_ref[...] * 2.0 + logw_ref[...]
    bias = offset - jnp.sum(y * y, axis=0, keepdims=True)
    out_ref[0:FEATURES, :] = (y * 2.0).astype(jnp.bfloat16)
    out_ref[FEATURES : FEATURES + EXTRA, :] = extra_block(
        three_parts(bias), ones_of(bias.shape[1])
    ).astype(jnp.bfloat16)
    offset_ref[...] = offset


def lay_sources(x_ref, xs_ref):
    per = x_ref.shape[2]
    for r in range(x_ref.shape[0]):
        xs_ref[0:FEATURES, r * per : (r + 1) * per] = x_ref[r]


def weights_at(xs_ref, at):
    part = xs_ref[:, at]
    rest = jnp.zeros((DEPTH - part.shape[0], part.shape[1]), part.dtype)
    return jnp.concatenate([part, rest], axis=0)


def product(a, b):
    return jnp.dot(a, b, preferred_element_type=jnp.float32)


def folded(value, combine):
    rows, n = value.shape
    return combine(value.reshape(rows // 8, 8, n), axis=0)


def join(a, b):
    top = jnp.maximum(a, b)
    return top + jnp.log(1.0 + jnp.exp(jnp.minimum(a, b) - top))


def first_kernel(last, *refs):
    y_ref, x_ref, refs = refs[0], refs[1], refs[2:]
    if last:
        before_ref, logw_ref, refs = refs[0], refs[1], refs[2:]
    yt_ref, l_ref, xs_ref, sums_ref = refs
    rows = yt_ref.shape[0]
    ny, _, per = x_ref.shape
    cols = ny * per
    wide = min(LANES, cols)
    row_step = min(STEP, rows)
    col_step = min(STEP, wide)

    extra = y_ref[FEATURES : FEATURES + EXTRA, :].astype(jnp.float32)
    bias = extra[0:1, :] + extra[1:2, :] + extra[2:3, :]
    shift = jnp.max(bias, axis=1, keepdims=True)
    for k in range(0, rows, row_step):
        block = jnp.concatenate(
            [
                y_ref[:, k : k + row_step].astype(jnp.float32),
                jnp.zeros((DEPTH - FEATURES - EXTRA, row_step), jnp.float32),
            ],
            axis=0,
        )
        yt_ref[k : k + row_step, :] = block.T.astype(jnp.bfloat16)
    lay_sources(x_ref, xs_ref)
    xs_ref[FEATURES : FEATURES + EXTRA, :] = extra_block(
        ones_of(cols), three_parts(jnp.broadcast_to(-shift, (1, cols)))
    ).astype(jnp.bfloat16)

    def store(row, value):
        if last:
            value = join(before_ref[row : row + 1, :], value)
        l_ref[row : row + 1, :] = value

    if last:
        l_ref[ny : ny + 1, :] = logw_ref[...]

    def main(g, carry):
        for t in range(wide // col_step):
            at = pl.ds(pl.multiple_of(g * wide + t * col_step, col_step), col_step)
            weights = weights_at(xs_ref, at)
            total = jnp.zeros((8, col_step), jnp.float32)
            for j in range(rows // row_step):
                score = product(yt_ref[j * row_step : (j + 1) * row_step, :], weights)
                total = total + folded(jnp.exp(score), jnp.sum)
            sums_ref[:, at] = total
        return carry

    lax.fori_loop(0, cols // wide, main, 0)
    total = jnp.sum(sums_ref[...], axis=0, keepdims=True)
    result = shift + jnp.log(total)
    for r in range(ny):
        store(r, result[:, r * per : (r + 1) * per])

    @pl.when(jnp.logical_not((jnp.min(total) > LOW) & (jnp.max(total) < HIGH)))
    def _():
        def again(g, carry):
            at = pl.ds(pl.multiple_of(g * col_step, col_step), col_step)
            weights = weights_at(xs_ref, at)

            def advance(j, state):
                top, total = state
                here = pl.ds(pl.multiple_of(j * row_step, row_step), row_step)
                score = product(yt_ref[here, :], weights)
                new = jnp.maximum(top, jnp.max(score, axis=0, keepdims=True))
                total = total * jnp.exp(top - new) + jnp.sum(
                    jnp.exp(score - new), axis=0, keepdims=True
                )
                return new, total

            start = (
                jnp.full((1, col_step), -1e30, jnp.float32),
                jnp.zeros((1, col_step), jnp.float32),
            )
            top, total = lax.fori_loop(0, rows // row_step, advance, start)
            sums_ref[0:1, at] = shift + top + jnp.log(total)
            return carry

        lax.fori_loop(0, cols // col_step, again, 0)
        for r in range(ny):
            store(r, sums_ref[0:1, r * per : (r + 1) * per])


def second_kernel(slots, place_ref, near_ref, far_ref, x_ref, c_ref, s_ref, xs_ref, left_ref, acc_ref, top_ref):
    nz, each = s_ref.shape
    rows = nz * each
    ny, _, per = x_ref.shape
    cols = ny * per
    row_step = each
    col_step = min(STEP, cols)

    lay_sources(x_ref, xs_ref)
    for r in range(ny):
        xs_ref[FEATURES : FEATURES + EXTRA, r * per : (r + 1) * per] = extra_block(
            ones_of(per), three_parts(c_ref[r : r + 1, :])
        ).astype(jnp.bfloat16)

    def lanes_folded(value, combine):
        out = value[:, 0:128]
        for k in range(1, value.shape[1] // 128):
            out = combine(out, value[:, k * 128 : (k + 1) * 128])
        return out

    for g, (half, k, _) in enumerate(slots):
        ref = far_ref if half else near_ref
        left_ref[g * each : (g + 1) * each, :] = ref[k * each : (k + 1) * each, :]

    def main(g, carry):
        here = pl.ds(pl.multiple_of(g * row_step, row_step), row_step)
        left = left_ref[here, :]
        total = jnp.zeros((row_step, 128), jnp.float32)
        for t in range(cols // col_step):
            score = product(
                left, weights_at(xs_ref, slice(t * col_step, (t + 1) * col_step))
            )
            total = total + lanes_folded(jnp.exp(score), jnp.add)
        acc_ref[here, :] = total
        return carry

    lax.fori_loop(0, rows // row_step, main, 0)

    def store(result):
        for g, (_, _, row) in enumerate(slots):
            s_ref[pl.ds(place_ref[0] ^ row, 1), :] = result[:, g * each : (g + 1) * each]

    total = jnp.sum(acc_ref[...].T, axis=0, keepdims=True)
    store(jnp.log(total))

    @pl.when(jnp.logical_not((jnp.min(total) > LOW) & (jnp.max(total) < HIGH)))
    def _():
        def again(g, carry):
            here = pl.ds(pl.multiple_of(g * row_step, row_step), row_step)
            left = left_ref[here, :]

            def advance(t, state):
                top, total = state
                at = pl.ds(pl.multiple_of(t * col_step, col_step), col_step)
                score = product(left, weights_at(xs_ref, at))
                new = jnp.maximum(top, lanes_folded(score, jnp.maximum))
                total = total * jnp.exp(top - new)
                for k in range(col_step // 128):
                    total = total + jnp.exp(score[:, k * 128 : (k + 1) * 128] - new)
                return new, total

            start = (
                jnp.full((row_step, 128), -1e30, jnp.float32),
                jnp.zeros((row_step, 128), jnp.float32),
            )
            top, total = lax.fori_loop(0, cols // col_step, advance, start)
            top_ref[here, :] = top
            acc_ref[here, :] = total
            return carry

        lax.fori_loop(0, rows // row_step, again, 0)
        tops = top_ref[...].T
        top = jnp.max(tops, axis=0, keepdims=True)
        total = jnp.sum(acc_ref[...].T * jnp.exp(tops - top), axis=0, keepdims=True)
        store(top + jnp.log(total))


def call(kernel, outs, scratch, flops, exps, *args, scalars=()):
    return pl.pallas_call(
        kernel,
        out_shape=outs,
        in_specs=[
            pl.BlockSpec(memory_space=pltpu.SMEM if k in scalars else pltpu.VMEM)
            for k in range(len(args))
        ],
        scratch_shapes=scratch,
        compiler_params=pltpu.CompilerParams(vmem_limit_bytes=40 * 2**20),
        cost_estimate=pl.CostEstimate(
            flops=flops, bytes_accessed=4 * 2**20, transcendentals=exps
        ),
    )(*args)


def log_sum(parts):
    top = jnp.max(parts, axis=0)
    return top + jnp.log(jnp.sum(jnp.exp(parts - top), axis=0))


def per_device(nz, ny, nw, source_latent, source_logw, target_latent, target_logw, target_potential):
    f32, bf16 = jnp.float32, jnp.bfloat16
    per = source_latent.shape[0]
    each = target_latent.shape[0]
    cols, half = ny * per, nz // 2 * each
    pairs = cols * half
    place = lax.axis_index("blk")
    my_y, my_z = place // nz, place % nz
    depth = FEATURES + EXTRA
    y_groups = [[y * nz + z for y in range(ny)] for z in range(nz)]
    quarters = [[g * (nz // 2) + z for z in range(nz // 2)] for g in range(2 * ny)]
    nx = nw // 4
    x_groups = [[(h * nx + x) * 2 + k for x in range(nx)] for h in range(2) for k in range(2)]

    def along_z(value, k):
        perm = [(y * nz + z, y * nz + (z ^ k)) for y in range(ny) for z in range(nz)]
        return lax.ppermute(value, "blk", perm)

    def along_wide(value, k):
        return lax.ppermute(value, "wide", [(w, w ^ k) for w in range(nw)])

    def shared(value, axis, groups):
        spread = jnp.broadcast_to(value[None], (len(groups[0]),) + value.shape)
        return lax.all_to_all(spread, axis, 0, 0, axis_index_groups=groups, tiled=True)

    def over_y(value):
        return shared(value, "blk", y_groups)

    y, offset = call(
        prepare_kernel,
        (jax.ShapeDtypeStruct((depth, each), bf16), jax.ShapeDtypeStruct((1, each), f32)),
        [],
        each * FEATURES * 4,
        0,
        target_latent.T,
        target_logw.reshape(1, each),
        target_potential.reshape(1, each),
    )
    x = source_latent.T
    xs = over_y(x)
    bit = nz // 2
    while bit > 1:
        y = jnp.concatenate([y, along_z(y, bit)], axis=1)
        bit //= 2
    xs, y = lax.optimization_barrier((xs, y))
    far = along_z(y, 1)

    def first(block, *more):
        last = len(more) > 0
        return call(
            functools.partial(first_kernel, last),
            (
                jax.ShapeDtypeStruct((half, DEPTH), bf16),
                jax.ShapeDtypeStruct((ny + last, per), f32),
            ),
            [pltpu.VMEM((depth, cols), bf16), pltpu.VMEM((8, cols), f32)],
            2 * pairs * DEPTH,
            pairs,
            block,
            xs,
            *more,
        )

    yt_near, total = first(y)
    yt_far, total = first(far, total, source_logw.reshape(1, per))
    got = over_y(total)
    total, logw = log_sum(got[:, :ny]), got[:, ny]
    total = log_sum(shared(total, "wide", x_groups))
    total = join(total, along_wide(total, 1))
    total = join(total, along_wide(total, nw // 2))
    c = logw - total
    sq = jnp.sum(jnp.square(x.astype(f32)), axis=0, keepdims=True)
    mine = lax.dynamic_slice(total, (my_y, 0), (1, per))
    source_potential = -0.5 * (mine - sq)

    count = nz // 2
    width = count.bit_length() - 1
    blocks = []
    for h in range(2):
        for k in range(count):
            away = 2 * int(format(k, "b").zfill(width)[::-1], 2) + h
            blocks.append((h, k, away))
    place_in = (my_z % count).astype(jnp.int32).reshape(1)

    def second(slots, near):
        return call(
            functools.partial(second_kernel, slots),
            jax.ShapeDtypeStruct((count, each), f32),
            [
                pltpu.VMEM((depth, cols), bf16),
                pltpu.VMEM((half, DEPTH), bf16),
                pltpu.VMEM((half, 128), f32),
                pltpu.VMEM((half, 128), f32),
            ],
            2 * pairs * DEPTH,
            pairs,
            place_in,
            near,
            yt_far,
            xs,
            c,
            scalars=(0,),
        )

    sent = second(tuple((h, k, a - count) for h, k, a in blocks if a >= count), yt_near)
    yt_near, sent = lax.optimization_barrier((yt_near, sent))
    other = along_z(sent, count)
    sums = join(second(tuple(b for b in blocks if b[2] < count), yt_near), other)
    sums = lax.all_to_all(sums, "blk", 0, 0, axis_index_groups=quarters, tiled=True)
    new_target_potential = -0.5 * (log_sum(sums) - offset[0])
    return source_potential.reshape(per), new_target_potential


def solution(mesh):
    nz = ZRUN
    ny = mesh.shape["blk"] // nz
    nw = mesh.shape["wide"]
    placed = (
        P("blk", None),
        P("blk"),
        P(("wide", "blk"), None),
        P(("wide", "blk")),
        P(("wide", "blk")),
    )
    return jax.shard_map(
        functools.partial(per_device, nz, ny, nw),
        mesh=mesh,
        in_specs=placed,
        out_specs=(P("blk"), P(("wide", "blk"))),
        check_vma=False,
    )
```

```python
import functools

import jax
import jax.numpy as jnp
from jax import lax
from jax.experimental import pallas as pl
from jax.experimental.pallas import tpu as pltpu
from jax.sharding import PartitionSpec as P

ZRUN = 8
FEATURES = 64
EXTRA = 16
DEPTH = 128
ROWS = 512
LANES = 256
LOW = 2.0**-60
HIGH = 2.0**120


def three_parts(value):
    high = value.astype(jnp.bfloat16).astype(jnp.float32)
    rest = value - high
    middle = rest.astype(jnp.bfloat16).astype(jnp.float32)
    low = (rest - middle).astype(jnp.bfloat16).astype(jnp.float32)
    return high, middle, low


def extra_block(first, second):
    n = first[0].shape[1]
    row = lax.broadcasted_iota(jnp.int32, (EXTRA, n), 0)
    block = jnp.zeros((EXTRA, n), jnp.float32)
    for k, part in enumerate(tuple(first) + tuple(second)):
        block = jnp.where(row == k, part, block)
    return block


def ones_of(n):
    one = jnp.ones((1, n), jnp.float32)
    return one, one, one


def prepare_kernel(y_ref, logw_ref, potential_ref, out_ref, offset_ref):
    y = y_ref[...].astype(jnp.float32)
    offset = potential_ref[...] * 2.0 + logw_ref[...]
    bias = offset - jnp.sum(y * y, axis=0, keepdims=True)
    out_ref[0:FEATURES, :] = (y * 2.0).astype(jnp.bfloat16)
    out_ref[FEATURES : FEATURES + EXTRA, :] = extra_block(
        three_parts(bias), ones_of(bias.shape[1])
    ).astype(jnp.bfloat16)
    offset_ref[...] = offset


def weights_of(features, extra):
    rest = jnp.zeros((DEPTH - FEATURES - EXTRA, features.shape[1]), features.dtype)
    return jnp.concatenate([features, extra, rest], axis=0)


def product(a, b):
    return jnp.dot(a, b, preferred_element_type=jnp.float32)


def folded(value, combine):
    rows, n = value.shape
    return combine(value.reshape(rows // 8, 8, n), axis=0)


def join(a, b):
    top = jnp.maximum(a, b)
    return top + jnp.log(1.0 + jnp.exp(jnp.minimum(a, b) - top))


def first_kernel(last, *refs):
    y_ref, x_ref, refs = refs[0], refs[1], refs[2:]
    if last:
        before_ref, logw_ref, refs = refs[0], refs[1], refs[2:]
    yt_ref, l_ref, sums_ref = refs
    rows = yt_ref.shape[0]
    ny, _, per = x_ref.shape
    row_step = min(ROWS, rows)
    col_step = min(LANES, per)
    together = 2

    extra = y_ref[FEATURES : FEATURES + EXTRA, :].astype(jnp.float32)
    bias = extra[0:1, :] + extra[1:2, :] + extra[2:3, :]
    shift = jnp.max(bias, axis=1, keepdims=True)
    for k in range(0, rows, row_step):
        block = jnp.concatenate(
            [
                y_ref[:, k : k + row_step].astype(jnp.float32),
                jnp.zeros((DEPTH - FEATURES - EXTRA, row_step), jnp.float32),
            ],
            axis=0,
        )
        yt_ref[k : k + row_step, :] = block.T.astype(jnp.bfloat16)
    extra = extra_block(
        ones_of(col_step), three_parts(jnp.broadcast_to(-shift, (1, col_step)))
    ).astype(jnp.bfloat16)

    def store(row, value):
        if last:
            value = join(before_ref[row : row + 1, :], value)
        l_ref[row : row + 1, :] = value

    if last:
        l_ref[ny : ny + 1, :] = logw_ref[...]

    def main(g, carry):
        for s in range(together):
            r = g * together + s
            for t in range(0, per, col_step):
                weights = weights_of(x_ref[r, :, t : t + col_step], extra)
                total = jnp.zeros((8, col_step), jnp.float32)
                for j in range(0, rows, row_step):
                    score = product(yt_ref[j : j + row_step, :], weights)
                    total = total + folded(jnp.exp(score), jnp.sum)
                sums_ref[r, :, t : t + col_step] = total
        return carry

    lax.fori_loop(0, ny // together, main, 0)
    total = jnp.sum(sums_ref[...], axis=1)
    result = shift + jnp.log(total)
    for r in range(ny):
        store(r, result[r : r + 1, :])

    @pl.when(jnp.logical_not((jnp.min(total) > LOW) & (jnp.max(total) < HIGH)))
    def _():
        def again(g, carry):
            at = pl.ds(pl.multiple_of(g * col_step, col_step), col_step)
            for r in range(ny):
                weights = weights_of(x_ref[r, :, at], extra)

                def advance(j, state):
                    top, total = state
                    here = pl.ds(pl.multiple_of(j * row_step, row_step), row_step)
                    score = product(yt_ref[here, :], weights)
                    new = jnp.maximum(top, jnp.max(score, axis=0, keepdims=True))
                    total = total * jnp.exp(top - new) + jnp.sum(
                        jnp.exp(score - new), axis=0, keepdims=True
                    )
                    return new, total

                start = (
                    jnp.full((1, col_step), -1e30, jnp.float32),
                    jnp.zeros((1, col_step), jnp.float32),
                )
                top, total = lax.fori_loop(0, rows // row_step, advance, start)
                sums_ref[r, 0:1, at] = shift + top + jnp.log(total)
            return carry

        lax.fori_loop(0, per // col_step, again, 0)
        for r in range(ny):
            store(r, sums_ref[r, 0:1, :])


def second_kernel(
    slots, place_ref, near_ref, far_ref, x_ref, c_ref, s_ref, extra_ref, left_ref, acc_ref, top_ref
):
    nz, each = s_ref.shape
    rows = nz * each
    ny, _, per = x_ref.shape
    row_step = min(ROWS, rows)
    col_step = min(LANES, per)

    for r in range(ny):
        extra_ref[r] = extra_block(
            ones_of(per), three_parts(c_ref[r : r + 1, :])
        ).astype(jnp.bfloat16)
    for g, (half, k, _) in enumerate(slots):
        ref = far_ref if half else near_ref
        left_ref[g * each : (g + 1) * each, :] = ref[k * each : (k + 1) * each, :]

    def lanes_folded(value, combine):
        out = value[:, 0:128]
        for k in range(1, value.shape[1] // 128):
            out = combine(out, value[:, k * 128 : (k + 1) * 128])
        return out

    def main(g, carry):
        here = pl.ds(pl.multiple_of(g * row_step, row_step), row_step)
        left = left_ref[here, :]
        for r in range(ny):
            for t in range(0, per, col_step):
                at = slice(t, t + col_step)
                score = product(left, weights_of(x_ref[r, :, at], extra_ref[r, :, at]))
                part = lanes_folded(jnp.exp(score), jnp.add)
                if r == 0 and t == 0:
                    acc_ref[here, :] = part
                else:
                    acc_ref[here, :] = acc_ref[here, :] + part
        return carry

    lax.fori_loop(0, rows // row_step, main, 0)

    def store(result):
        for g, (_, _, row) in enumerate(slots):
            s_ref[pl.ds(place_ref[0] ^ row, 1), :] = result[:, g * each : (g + 1) * each]

    total = jnp.sum(acc_ref[...].T, axis=0, keepdims=True)
    store(jnp.log(total))

    @pl.when(jnp.logical_not((jnp.min(total) > LOW) & (jnp.max(total) < HIGH)))
    def _():
        def again(g, carry):
            here = pl.ds(pl.multiple_of(g * each, each), each)
            left = left_ref[here, :]
            state = (
                jnp.full((each, 128), -1e30, jnp.float32),
                jnp.zeros((each, 128), jnp.float32),
            )
            for r in range(ny):

                def advance(t, state):
                    top, total = state
                    at = pl.ds(pl.multiple_of(t * col_step, col_step), col_step)
                    score = product(left, weights_of(x_ref[r, :, at], extra_ref[r, :, at]))
                    new = jnp.maximum(top, lanes_folded(score, jnp.maximum))
                    total = total * jnp.exp(top - new)
                    for k in range(col_step // 128):
                        total = total + jnp.exp(score[:, k * 128 : (k + 1) * 128] - new)
                    return new, total

                state = lax.fori_loop(0, per // col_step, advance, state)
            top_ref[here, :] = state[0]
            acc_ref[here, :] = state[1]
            return carry

        lax.fori_loop(0, rows // each, again, 0)
        tops = top_ref[...].T
        top = jnp.max(tops, axis=0, keepdims=True)
        total = jnp.sum(acc_ref[...].T * jnp.exp(tops - top), axis=0, keepdims=True)
        store(top + jnp.log(total))


def call(kernel, outs, scratch, flops, exps, *args, spaces=None):
    return pl.pallas_call(
        kernel,
        out_shape=outs,
        in_specs=[
            pl.BlockSpec(memory_space=space) for space in spaces or [pltpu.VMEM] * len(args)
        ],
        scratch_shapes=scratch,
        compiler_params=pltpu.CompilerParams(vmem_limit_bytes=40 * 2**20),
        cost_estimate=pl.CostEstimate(
            flops=flops, bytes_accessed=4 * 2**20, transcendentals=exps
        ),
    )(*args)


def log_sum(parts):
    top = jnp.max(parts, axis=0)
    return top + jnp.log(jnp.sum(jnp.exp(parts - top), axis=0))


def per_device(nz, ny, nw, source_latent, source_logw, target_latent, target_logw, target_potential):
    f32, bf16 = jnp.float32, jnp.bfloat16
    per = source_latent.shape[0]
    each = target_latent.shape[0]
    cols, half = ny * per, nz // 2 * each
    pairs = cols * half
    place = lax.axis_index("blk")
    my_y, my_z = place // nz, place % nz
    depth = FEATURES + EXTRA
    y_groups = [[y * nz + z for y in range(ny)] for z in range(nz)]
    quarters = [[g * (nz // 2) + z for z in range(nz // 2)] for g in range(2 * ny)]
    nx = nw // 4
    x_groups = [[(h * nx + x) * 2 + k for x in range(nx)] for h in range(2) for k in range(2)]

    def along_z(value, k):
        perm = [(y * nz + z, y * nz + (z ^ k)) for y in range(ny) for z in range(nz)]
        return lax.ppermute(value, "blk", perm)

    def along_wide(value, k):
        return lax.ppermute(value, "wide", [(w, w ^ k) for w in range(nw)])

    def shared(value, axis, groups):
        spread = jnp.broadcast_to(value[None], (len(groups[0]),) + value.shape)
        return lax.all_to_all(spread, axis, 0, 0, axis_index_groups=groups, tiled=True)

    y, offset = call(
        prepare_kernel,
        (jax.ShapeDtypeStruct((depth, each), bf16), jax.ShapeDtypeStruct((1, each), f32)),
        [],
        each * FEATURES * 4,
        0,
        target_latent.T,
        target_logw.reshape(1, each),
        target_potential.reshape(1, each),
    )
    x = source_latent.T
    xs = shared(x, "blk", y_groups)
    bit = nz // 2
    while bit > 1:
        y = jnp.concatenate([y, along_z(y, bit)], axis=1)
        bit //= 2
    xs, y = lax.optimization_barrier((xs, y))
    far = along_z(y, 1)

    def first(block, *more):
        last = len(more) > 0
        return call(
            functools.partial(first_kernel, last),
            (
                jax.ShapeDtypeStruct((half, DEPTH), bf16),
                jax.ShapeDtypeStruct((ny + last, per), f32),
            ),
            [pltpu.VMEM((ny, 8, per), f32)],
            2 * pairs * DEPTH,
            pairs,
            block,
            xs,
            *more,
        )

    yt_near, total = first(y)
    yt_far, total = first(far, total, source_logw.reshape(1, per))
    got = shared(total, "blk", y_groups)
    total, logw = log_sum(got[:, :ny]), got[:, ny]
    total = log_sum(shared(total, "wide", x_groups))
    total = join(total, along_wide(total, 1))
    total = join(total, along_wide(total, nw // 2))
    c = logw - total
    sq = jnp.sum(jnp.square(x.astype(f32)), axis=0, keepdims=True)
    mine = lax.dynamic_slice(total, (my_y, 0), (1, per))
    source_potential = -0.5 * (mine - sq)

    count = nz // 2
    width = count.bit_length() - 1
    blocks = []
    for h in range(2):
        for k in range(count):
            away = 2 * int(format(k, "b").zfill(width)[::-1], 2) + h
            blocks.append((h, k, away))
    place_in = (my_z % count).astype(jnp.int32).reshape(1)

    def second(slots, near):
        return call(
            functools.partial(second_kernel, slots),
            jax.ShapeDtypeStruct((count, each), f32),
            [
                pltpu.VMEM((ny, EXTRA, per), bf16),
                pltpu.VMEM((half, DEPTH), bf16),
                pltpu.VMEM((half, 128), f32),
                pltpu.VMEM((half, 128), f32),
            ],
            2 * pairs * DEPTH,
            pairs,
            place_in,
            near,
            yt_far,
            xs,
            c,
            spaces=[pltpu.SMEM] + [pltpu.VMEM] * 4,
        )

    sent = second(tuple((h, k, a - count) for h, k, a in blocks if a >= count), yt_near)
    yt_near, sent = lax.optimization_barrier((yt_near, sent))
    other = along_z(sent, count)
    sums = join(second(tuple(b for b in blocks if b[2] < count), yt_near), other)
    sums = lax.all_to_all(sums, "blk", 0, 0, axis_index_groups=quarters, tiled=True)
    new_target_potential = -0.5 * (log_sum(sums) - offset[0])
    return source_potential.reshape(per), new_target_potential


def solution(mesh):
    nz = ZRUN
    ny = mesh.shape["blk"] // nz
    nw = mesh.shape["wide"]
    placed = (
        P("blk", None),
        P("blk"),
        P(("wide", "blk"), None),
        P(("wide", "blk")),
        P(("wide", "blk")),
    )
    return jax.shard_map(
        functools.partial(per_device, nz, ny, nw),
        mesh=mesh,
        in_specs=placed,
        out_specs=(P("blk"), P(("wide", "blk"))),
        check_vma=False,
    )
```

```python
import functools

import jax
import jax.numpy as jnp
from jax import lax
from jax.experimental import pallas as pl
from jax.experimental.pallas import tpu as pltpu
from jax.sharding import PartitionSpec as P

ZRUN = 8
FEATURES = 64
EXTRA = 16
DEPTH = 128
ROWS = 512
LANES = 256
LOW = 2.0**-60
HIGH = 2.0**120


def three_parts(value):
    high = value.astype(jnp.bfloat16).astype(jnp.float32)
    rest = value - high
    middle = rest.astype(jnp.bfloat16).astype(jnp.float32)
    low = (rest - middle).astype(jnp.bfloat16).astype(jnp.float32)
    return high, middle, low


def extra_block(first, second):
    n = first[0].shape[1]
    row = lax.broadcasted_iota(jnp.int32, (EXTRA, n), 0)
    block = jnp.zeros((EXTRA, n), jnp.float32)
    for k, part in enumerate(tuple(first) + tuple(second)):
        block = jnp.where(row == k, part, block)
    return block


def ones_of(n):
    one = jnp.ones((1, n), jnp.float32)
    return one, one, one


def prepare_kernel(y_ref, logw_ref, potential_ref, out_ref, offset_ref):
    y = y_ref[...].astype(jnp.float32)
    offset = potential_ref[...] * 2.0 + logw_ref[...]
    bias = offset - jnp.sum(y * y, axis=0, keepdims=True)
    out_ref[0:FEATURES, :] = (y * 2.0).astype(jnp.bfloat16)
    out_ref[FEATURES : FEATURES + EXTRA, :] = extra_block(
        three_parts(bias), ones_of(bias.shape[1])
    ).astype(jnp.bfloat16)
    offset_ref[...] = offset


def weights_of(features, extra):
    rest = jnp.zeros((DEPTH - FEATURES - EXTRA, features.shape[1]), features.dtype)
    return jnp.concatenate([features, extra, rest], axis=0)


def product(a, b):
    return jnp.dot(a, b, preferred_element_type=jnp.float32)


def folded(value, combine):
    rows, n = value.shape
    return combine(value.reshape(rows // 8, 8, n), axis=0)


def join(a, b):
    top = jnp.maximum(a, b)
    return top + jnp.log(1.0 + jnp.exp(jnp.minimum(a, b) - top))


def first_kernel(last, *refs):
    y_ref, x_ref, refs = refs[0], refs[1], refs[2:]
    if last:
        before_ref, logw_ref, refs = refs[0], refs[1], refs[2:]
    yt_ref, l_ref, sums_ref = refs
    rows = yt_ref.shape[0]
    ny, _, per = x_ref.shape
    row_step = min(ROWS, rows)
    col_step = min(LANES, per)
    together = 2

    extra = y_ref[FEATURES : FEATURES + EXTRA, :].astype(jnp.float32)
    bias = extra[0:1, :] + extra[1:2, :] + extra[2:3, :]
    shift = jnp.max(bias, axis=1, keepdims=True)
    for k in range(0, rows, row_step):
        block = jnp.concatenate(
            [
                y_ref[:, k : k + row_step].astype(jnp.float32),
                jnp.zeros((DEPTH - FEATURES - EXTRA, row_step), jnp.float32),
            ],
            axis=0,
        )
        yt_ref[k : k + row_step, :] = block.T.astype(jnp.bfloat16)
    extra = extra_block(
        ones_of(col_step), three_parts(jnp.broadcast_to(-shift, (1, col_step)))
    ).astype(jnp.bfloat16)

    def store(row, value):
        if last:
            value = join(before_ref[row : row + 1, :], value)
        l_ref[row : row + 1, :] = value

    if last:
        l_ref[ny : ny + 1, :] = logw_ref[...]

    def main(g, carry):
        for s in range(together):
            r = g * together + s
            for t in range(0, per, col_step):
                weights = weights_of(x_ref[r, :, t : t + col_step], extra)
                total = jnp.zeros((8, col_step), jnp.float32)
                for j in range(0, rows, row_step):
                    score = product(yt_ref[j : j + row_step, :], weights)
                    total = total + folded(jnp.exp(score), jnp.sum)
                sums_ref[r, :, t : t + col_step] = total
        return carry

    lax.fori_loop(0, ny // together, main, 0)
    total = jnp.sum(sums_ref[...], axis=1)
    result = shift + jnp.log(total)
    for r in range(ny):
        store(r, result[r : r + 1, :])

    @pl.when(jnp.logical_not((jnp.min(total) > LOW) & (jnp.max(total) < HIGH)))
    def _():
        def again(g, carry):
            at = pl.ds(pl.multiple_of(g * col_step, col_step), col_step)
            for r in range(ny):
                weights = weights_of(x_ref[r, :, at], extra)

                def advance(j, state):
                    top, total = state
                    here = pl.ds(pl.multiple_of(j * row_step, row_step), row_step)
                    score = product(yt_ref[here, :], weights)
                    new = jnp.maximum(top, jnp.max(score, axis=0, keepdims=True))
                    total = total * jnp.exp(top - new) + jnp.sum(
                        jnp.exp(score - new), axis=0, keepdims=True
                    )
                    return new, total

                start = (
                    jnp.full((1, col_step), -1e30, jnp.float32),
                    jnp.zeros((1, col_step), jnp.float32),
                )
                top, total = lax.fori_loop(0, rows // row_step, advance, start)
                sums_ref[r, 0:1, at] = shift + top + jnp.log(total)
            return carry

        lax.fori_loop(0, per // col_step, again, 0)
        for r in range(ny):
            store(r, sums_ref[r, 0:1, :])


def second_kernel(
    slots, place_ref, near_ref, far_ref, x_ref, c_ref, s_ref, extra_ref, left_ref, acc_ref, top_ref
):
    nz, _, each = s_ref.shape
    rows = nz * each
    ny, _, per = x_ref.shape
    row_step = min(ROWS, rows)
    col_step = min(LANES, per)

    for r in range(ny):
        extra_ref[r] = extra_block(
            ones_of(per), three_parts(c_ref[r : r + 1, :])
        ).astype(jnp.bfloat16)
    for g, (half, k, _) in enumerate(slots):
        ref = far_ref if half else near_ref
        left_ref[g * each : (g + 1) * each, :] = ref[k * each : (k + 1) * each, :]

    def lanes_folded(value, combine):
        out = value[:, 0:128]
        for k in range(1, value.shape[1] // 128):
            out = combine(out, value[:, k * 128 : (k + 1) * 128])
        return out

    def main(g, carry):
        here = pl.ds(pl.multiple_of(g * row_step, row_step), row_step)
        left = left_ref[here, :]
        for r in range(ny):
            for t in range(0, per, col_step):
                at = slice(t, t + col_step)
                score = product(left, weights_of(x_ref[r, :, at], extra_ref[r, :, at]))
                part = lanes_folded(jnp.exp(score), jnp.add)
                if r == 0 and t == 0:
                    acc_ref[here, :] = part
                else:
                    acc_ref[here, :] = acc_ref[here, :] + part
        return carry

    lax.fori_loop(0, rows // row_step, main, 0)

    def store(result):
        for g, (_, _, row) in enumerate(slots):
            s_ref[place_ref[0] ^ row] = result[:, g * each : (g + 1) * each]

    total = jnp.sum(acc_ref[...].T, axis=0, keepdims=True)
    store(jnp.log(total))

    @pl.when(jnp.logical_not((jnp.min(total) > LOW) & (jnp.max(total) < HIGH)))
    def _():
        def again(g, carry):
            here = pl.ds(pl.multiple_of(g * each, each), each)
            left = left_ref[here, :]
            state = (
                jnp.full((each, 128), -1e30, jnp.float32),
                jnp.zeros((each, 128), jnp.float32),
            )
            for r in range(ny):

                def advance(t, state):
                    top, total = state
                    at = pl.ds(pl.multiple_of(t * col_step, col_step), col_step)
                    score = product(left, weights_of(x_ref[r, :, at], extra_ref[r, :, at]))
                    new = jnp.maximum(top, lanes_folded(score, jnp.maximum))
                    total = total * jnp.exp(top - new)
                    for k in range(col_step // 128):
                        total = total + jnp.exp(score[:, k * 128 : (k + 1) * 128] - new)
                    return new, total

                state = lax.fori_loop(0, per // col_step, advance, state)
            top_ref[here, :] = state[0]
            acc_ref[here, :] = state[1]
            return carry

        lax.fori_loop(0, rows // each, again, 0)
        tops = top_ref[...].T
        top = jnp.max(tops, axis=0, keepdims=True)
        total = jnp.sum(acc_ref[...].T * jnp.exp(tops - top), axis=0, keepdims=True)
        store(top + jnp.log(total))


def call(kernel, outs, scratch, flops, exps, *args, spaces=None):
    return pl.pallas_call(
        kernel,
        out_shape=outs,
        in_specs=[
            pl.BlockSpec(memory_space=space) for space in spaces or [pltpu.VMEM] * len(args)
        ],
        scratch_shapes=scratch,
        compiler_params=pltpu.CompilerParams(vmem_limit_bytes=40 * 2**20),
        cost_estimate=pl.CostEstimate(
            flops=flops, bytes_accessed=4 * 2**20, transcendentals=exps
        ),
    )(*args)


def log_sum(parts):
    top = jnp.max(parts, axis=0)
    return top + jnp.log(jnp.sum(jnp.exp(parts - top), axis=0))


def per_device(nz, ny, nw, source_latent, source_logw, target_latent, target_logw, target_potential):
    f32, bf16 = jnp.float32, jnp.bfloat16
    per = source_latent.shape[0]
    each = target_latent.shape[0]
    cols, half = ny * per, nz // 2 * each
    pairs = cols * half
    place = lax.axis_index("blk")
    my_y, my_z = place // nz, place % nz
    depth = FEATURES + EXTRA
    y_groups = [[y * nz + z for y in range(ny)] for z in range(nz)]
    z_groups = [[y * nz + z for z in range(nz)] for y in range(ny)]
    x_groups = [[h * (nw // 2) + k for k in range(nw // 2)] for h in range(2)]

    def along_z(value, k):
        perm = [(y * nz + z, y * nz + (z ^ k)) for y in range(ny) for z in range(nz)]
        return lax.ppermute(value, "blk", perm)

    def along_wide(value, k):
        return lax.ppermute(value, "wide", [(w, w ^ k) for w in range(nw)])

    def shared(value, axis, groups):
        spread = jnp.broadcast_to(value[None], (len(groups[0]),) + value.shape)
        return lax.all_to_all(spread, axis, 0, 0, axis_index_groups=groups, tiled=True)

    y, offset = call(
        prepare_kernel,
        (jax.ShapeDtypeStruct((depth, each), bf16), jax.ShapeDtypeStruct((1, each), f32)),
        [],
        each * FEATURES * 4,
        0,
        target_latent.T,
        target_logw.reshape(1, each),
        target_potential.reshape(1, each),
    )
    x = source_latent.T
    xs = shared(x, "blk", y_groups)
    bit = nz // 2
    while bit > 1:
        y = jnp.concatenate([y, along_z(y, bit)], axis=1)
        bit //= 2
    far = along_z(y, 1)

    def first(block, *more):
        last = len(more) > 0
        return call(
            functools.partial(first_kernel, last),
            (
                jax.ShapeDtypeStruct((half, DEPTH), bf16),
                jax.ShapeDtypeStruct((ny + last, per), f32),
            ),
            [pltpu.VMEM((ny, 8, per), f32)],
            2 * pairs * DEPTH,
            pairs,
            block,
            xs,
            *more,
        )

    yt_near, total = first(y)
    yt_far, total = first(far, total, source_logw.reshape(1, per))
    got = shared(total, "blk", y_groups)
    total, logw = log_sum(got[:, :ny]), got[:, ny]
    total = log_sum(shared(total, "wide", x_groups))
    total = join(total, along_wide(total, nw // 2))
    c = logw - total
    sq = jnp.sum(jnp.square(x.astype(f32)), axis=0, keepdims=True)
    mine = lax.dynamic_slice(total, (my_y, 0), (1, per))
    source_potential = -0.5 * (mine - sq)

    count = nz // 2
    width = count.bit_length() - 1
    slots = []
    for h in range(2):
        for k in range(count):
            slots.append((h, k, 2 * int(format(k, "b").zfill(width)[::-1], 2) + h))
    rows = nz * each
    sums = call(
        functools.partial(second_kernel, slots),
        jax.ShapeDtypeStruct((nz, 1, each), f32),
        [
            pltpu.VMEM((ny, EXTRA, per), bf16),
            pltpu.VMEM((rows, DEPTH), bf16),
            pltpu.VMEM((rows, 128), f32),
            pltpu.VMEM((rows, 128), f32),
        ],
        2 * cols * rows * DEPTH,
        cols * rows,
        my_z.astype(jnp.int32).reshape(1),
        yt_near,
        yt_far,
        xs,
        c,
        spaces=[pltpu.SMEM] + [pltpu.VMEM] * 4,
    )
    sums = lax.all_to_all(sums, "blk", 0, 0, axis_index_groups=z_groups, tiled=True)
    new_target_potential = -0.5 * (log_sum(sums)[0] - offset[0])
    return source_potential.reshape(per), new_target_potential


def solution(mesh):
    nz = ZRUN
    ny = mesh.shape["blk"] // nz
    nw = mesh.shape["wide"]
    placed = (
        P("blk", None),
        P("blk"),
        P(("wide", "blk"), None),
        P(("wide", "blk")),
        P(("wide", "blk")),
    )
    return jax.shard_map(
        functools.partial(per_device, nz, ny, nw),
        mesh=mesh,
        in_specs=placed,
        out_specs=(P("blk"), P(("wide", "blk"))),
        check_vma=False,
    )
```

```python
import functools

import jax
import jax.numpy as jnp
from jax import lax
from jax.experimental import pallas as pl
from jax.experimental.pallas import tpu as pltpu
from jax.sharding import PartitionSpec as P

ZRUN = 8
FEATURES = 64
EXTRA = 16
DEPTH = 128
ROWS = 512
LANES = 256
LOW = 2.0**-60
HIGH = 2.0**120


def three_parts(value):
    high = value.astype(jnp.bfloat16).astype(jnp.float32)
    rest = value - high
    middle = rest.astype(jnp.bfloat16).astype(jnp.float32)
    low = (rest - middle).astype(jnp.bfloat16).astype(jnp.float32)
    return high, middle, low


def extra_block(first, second):
    n = first[0].shape[1]
    row = lax.broadcasted_iota(jnp.int32, (EXTRA, n), 0)
    block = jnp.zeros((EXTRA, n), jnp.float32)
    for k, part in enumerate(tuple(first) + tuple(second)):
        block = jnp.where(row == k, part, block)
    return block


def ones_of(n):
    one = jnp.ones((1, n), jnp.float32)
    return one, one, one


def prepare_kernel(core_ref, y_ref, logw_ref, potential_ref, out_ref, offset_ref):
    y = y_ref[...].astype(jnp.float32)
    offset = potential_ref[...] * 2.0 + logw_ref[...]
    bias = offset - jnp.sum(y * y, axis=0, keepdims=True)
    half = FEATURES // 2
    first, second = y[0:half, :] * 2.0, y[half:FEATURES, :] * 2.0
    swap = core_ref[0] != 0
    out_ref[0:half, :] = jnp.where(swap, second, first).astype(jnp.bfloat16)
    out_ref[half:FEATURES, :] = jnp.where(swap, first, second).astype(jnp.bfloat16)
    out_ref[FEATURES : FEATURES + EXTRA, :] = extra_block(
        three_parts(bias), ones_of(bias.shape[1])
    ).astype(jnp.bfloat16)
    offset_ref[...] = offset


def weights_of(own_ref, other_ref, r, at, extra):
    rest = jnp.zeros((DEPTH - FEATURES - EXTRA, extra.shape[1]), extra.dtype)
    return jnp.concatenate([own_ref[r, :, at], other_ref[r, :, at], extra, rest], axis=0)


def product(a, b):
    return jnp.dot(a, b, preferred_element_type=jnp.float32)


def folded(value, combine):
    rows, n = value.shape
    return combine(value.reshape(rows // 8, 8, n), axis=0)


def join(a, b):
    top = jnp.maximum(a, b)
    return top + jnp.log(1.0 + jnp.exp(jnp.minimum(a, b) - top))


def first_kernel(last, *refs):
    y_ref, own_ref, other_ref, refs = refs[0], refs[1], refs[2], refs[3:]
    if last:
        before_ref, logw_ref, refs = refs[0], refs[1], refs[2:]
    yt_ref, l_ref, sums_ref = refs
    rows = yt_ref.shape[0]
    ny, _, per = own_ref.shape
    row_step = min(ROWS, rows)
    col_step = min(LANES, per)
    together = 2

    extra = y_ref[FEATURES : FEATURES + EXTRA, :].astype(jnp.float32)
    bias = extra[0:1, :] + extra[1:2, :] + extra[2:3, :]
    shift = jnp.max(bias, axis=1, keepdims=True)
    for k in range(0, rows, row_step):
        block = jnp.concatenate(
            [
                y_ref[:, k : k + row_step].astype(jnp.float32),
                jnp.zeros((DEPTH - FEATURES - EXTRA, row_step), jnp.float32),
            ],
            axis=0,
        )
        yt_ref[k : k + row_step, :] = block.T.astype(jnp.bfloat16)
    extra = extra_block(
        ones_of(col_step), three_parts(jnp.broadcast_to(-shift, (1, col_step)))
    ).astype(jnp.bfloat16)

    def store(row, value):
        if last:
            value = join(before_ref[row : row + 1, :], value)
        l_ref[row : row + 1, 0:per] = value

    if last:
        part = per // ny
        for k in range(ny):
            l_ref[k : k + 1, per:] = logw_ref[:, k * part : (k + 1) * part]

    def main(g, carry):
        for s in range(together):
            r = g * together + s
            for t in range(0, per, col_step):
                weights = weights_of(own_ref, other_ref, r, slice(t, t + col_step), extra)
                total = jnp.zeros((8, col_step), jnp.float32)
                for j in range(0, rows, row_step):
                    score = product(yt_ref[j : j + row_step, :], weights)
                    total = total + folded(jnp.exp(score), jnp.sum)
                sums_ref[r, :, t : t + col_step] = total
        return carry

    lax.fori_loop(0, ny // together, main, 0)
    total = jnp.sum(sums_ref[...], axis=1)
    result = shift + jnp.log(total)
    for r in range(ny):
        store(r, result[r : r + 1, :])

    @pl.when(jnp.logical_not((jnp.min(total) > LOW) & (jnp.max(total) < HIGH)))
    def _():
        def again(g, carry):
            at = pl.ds(pl.multiple_of(g * col_step, col_step), col_step)
            for r in range(ny):
                weights = weights_of(own_ref, other_ref, r, at, extra)

                def advance(j, state):
                    top, total = state
                    here = pl.ds(pl.multiple_of(j * row_step, row_step), row_step)
                    score = product(yt_ref[here, :], weights)
                    new = jnp.maximum(top, jnp.max(score, axis=0, keepdims=True))
                    total = total * jnp.exp(top - new) + jnp.sum(
                        jnp.exp(score - new), axis=0, keepdims=True
                    )
                    return new, total

                start = (
                    jnp.full((1, col_step), -1e30, jnp.float32),
                    jnp.zeros((1, col_step), jnp.float32),
                )
                top, total = lax.fori_loop(0, rows // row_step, advance, start)
                sums_ref[r, 0:1, at] = shift + top + jnp.log(total)
            return carry

        lax.fori_loop(0, per // col_step, again, 0)
        for r in range(ny):
            store(r, sums_ref[r, 0:1, :])


def second_kernel(
    slots,
    place_ref,
    near_ref,
    far_ref,
    own_ref,
    other_ref,
    total_ref,
    logw_ref,
    s_ref,
    extra_ref,
    left_ref,
    acc_ref,
    top_ref,
):
    nz, each = s_ref.shape
    rows = nz * each
    ny, _, per = own_ref.shape
    row_step = min(ROWS, rows)
    col_step = min(LANES, per)

    for r in range(ny):
        logw = jnp.concatenate([logw_ref[r, k : k + 1, per:] for k in range(ny)], axis=1)
        c = logw - total_ref[r : r + 1, :]
        extra_ref[r] = extra_block(ones_of(per), three_parts(c)).astype(jnp.bfloat16)
    for g, (half, k, _) in enumerate(slots):
        ref = far_ref if half else near_ref
        left_ref[g * each : (g + 1) * each, :] = ref[k * each : (k + 1) * each, :]

    def lanes_folded(value, combine):
        out = value[:, 0:128]
        for k in range(1, value.shape[1] // 128):
            out = combine(out, value[:, k * 128 : (k + 1) * 128])
        return out

    def main(g, carry):
        here = pl.ds(pl.multiple_of(g * row_step, row_step), row_step)
        left = left_ref[here, :]
        for r in range(ny):
            for t in range(0, per, col_step):
                at = slice(t, t + col_step)
                score = product(left, weights_of(own_ref, other_ref, r, at, extra_ref[r, :, at]))
                part = lanes_folded(jnp.exp(score), jnp.add)
                if r == 0 and t == 0:
                    acc_ref[here, :] = part
                else:
                    acc_ref[here, :] = acc_ref[here, :] + part
        return carry

    lax.fori_loop(0, rows // row_step, main, 0)

    def store(result):
        for g, (_, _, row) in enumerate(slots):
            s_ref[pl.ds(place_ref[0] ^ row, 1), :] = result[:, g * each : (g + 1) * each]

    total = jnp.sum(acc_ref[...].T, axis=0, keepdims=True)
    store(jnp.log(total))

    @pl.when(jnp.logical_not((jnp.min(total) > LOW) & (jnp.max(total) < HIGH)))
    def _():
        def again(g, carry):
            here = pl.ds(pl.multiple_of(g * each, each), each)
            left = left_ref[here, :]
            state = (
                jnp.full((each, 128), -1e30, jnp.float32),
                jnp.zeros((each, 128), jnp.float32),
            )
            for r in range(ny):

                def advance(t, state):
                    top, total = state
                    at = pl.ds(pl.multiple_of(t * col_step, col_step), col_step)
                    score = product(left, weights_of(own_ref, other_ref, r, at, extra_ref[r, :, at]))
                    new = jnp.maximum(top, lanes_folded(score, jnp.maximum))
                    total = total * jnp.exp(top - new)
                    for k in range(col_step // 128):
                        total = total + jnp.exp(score[:, k * 128 : (k + 1) * 128] - new)
                    return new, total

                state = lax.fori_loop(0, per // col_step, advance, state)
            top_ref[here, :] = state[0]
            acc_ref[here, :] = state[1]
            return carry

        lax.fori_loop(0, rows // each, again, 0)
        tops = top_ref[...].T
        top = jnp.max(tops, axis=0, keepdims=True)
        total = jnp.sum(acc_ref[...].T * jnp.exp(tops - top), axis=0, keepdims=True)
        store(top + jnp.log(total))


def call(kernel, outs, scratch, flops, exps, *args, spaces=None):
    return pl.pallas_call(
        kernel,
        out_shape=outs,
        in_specs=[
            pl.BlockSpec(memory_space=space) for space in spaces or [pltpu.VMEM] * len(args)
        ],
        scratch_shapes=scratch,
        compiler_params=pltpu.CompilerParams(vmem_limit_bytes=40 * 2**20),
        cost_estimate=pl.CostEstimate(
            flops=flops, bytes_accessed=4 * 2**20, transcendentals=exps
        ),
    )(*args)


def log_sum(parts):
    top = jnp.max(parts, axis=0)
    return top + jnp.log(jnp.sum(jnp.exp(parts - top), axis=0))


def per_device(nz, ny, nw, source_latent, source_logw, target_latent, target_logw, target_potential):
    f32, bf16 = jnp.float32, jnp.bfloat16
    per = source_latent.shape[0]
    each = target_latent.shape[0]
    cols, half = ny * per, nz // 2 * each
    pairs = cols * half
    place = lax.axis_index("blk")
    my_y, my_z = place // nz, place % nz
    core = (lax.axis_index("wide") % 2).astype(jnp.int32)
    depth = FEATURES + EXTRA
    y_groups = [[y * nz + z for y in range(ny)] for z in range(nz)]
    quarters = [[g * (nz // 2) + z for z in range(nz // 2)] for g in range(2 * ny)]
    x_groups = [[h * (nw // 2) + k for k in range(nw // 2)] for h in range(2)]

    def along_z(value, k):
        perm = [(y * nz + z, y * nz + (z ^ k)) for y in range(ny) for z in range(nz)]
        return lax.ppermute(value, "blk", perm)

    def along_wide(value, k):
        return lax.ppermute(value, "wide", [(w, w ^ k) for w in range(nw)])

    def shared(value, axis, groups):
        spread = jnp.broadcast_to(value[None], (len(groups[0]),) + value.shape)
        return lax.all_to_all(spread, axis, 0, 0, axis_index_groups=groups, tiled=True)

    y, offset = call(
        prepare_kernel,
        (jax.ShapeDtypeStruct((depth, each), bf16), jax.ShapeDtypeStruct((1, each), f32)),
        [],
        each * FEATURES * 4,
        0,
        core.reshape(1),
        target_latent.T,
        target_logw.reshape(1, each),
        target_potential.reshape(1, each),
        spaces=[pltpu.SMEM] + [pltpu.VMEM] * 3,
    )
    x = source_latent.T
    part = lax.dynamic_slice(x, (core * (FEATURES // 2), 0), (FEATURES // 2, per))
    own = shared(part, "blk", y_groups)
    bit = nz // 2
    while bit > 1:
        y = jnp.concatenate([y, along_z(y, bit)], axis=1)
        if bit == nz // 2:
            own, _ = lax.optimization_barrier((own, y))
            other = along_wide(own, 1)
        bit //= 2
    far = along_z(y, 1)

    def first(block, *more):
        last = len(more) > 0
        return call(
            functools.partial(first_kernel, last),
            (
                jax.ShapeDtypeStruct((half, DEPTH), bf16),
                jax.ShapeDtypeStruct((ny, per + per // ny if last else per), f32),
            ),
            [pltpu.VMEM((ny, 8, per), f32)],
            2 * pairs * DEPTH,
            pairs,
            block,
            own,
            other,
            *more,
        )

    yt_near, total = first(y)
    yt_far, total = first(far, total, source_logw.reshape(1, per))
    got = shared(total, "blk", y_groups)
    total = log_sum(got[:, :, :per])
    total = log_sum(shared(total, "wide", x_groups))
    total = join(total, along_wide(total, nw // 2))
    sq = jnp.sum(jnp.square(x.astype(f32)), axis=0, keepdims=True)
    mine = lax.dynamic_slice(total, (my_y, 0), (1, per))
    source_potential = -0.5 * (mine - sq)

    count = nz // 2
    width = count.bit_length() - 1
    blocks = []
    for h in range(2):
        for k in range(count):
            blocks.append((h, k, 2 * int(format(k, "b").zfill(width)[::-1], 2) + h))
    place_in = (my_z % count).astype(jnp.int32).reshape(1)

    def second(slots, near):
        return call(
            functools.partial(second_kernel, slots),
            jax.ShapeDtypeStruct((count, each), f32),
            [
                pltpu.VMEM((ny, EXTRA, per), bf16),
                pltpu.VMEM((half, DEPTH), bf16),
                pltpu.VMEM((half, 128), f32),
                pltpu.VMEM((half, 128), f32),
            ],
            2 * pairs * DEPTH,
            pairs,
            place_in,
            near,
            yt_far,
            own,
            other,
            total,
            got,
            spaces=[pltpu.SMEM] + [pltpu.VMEM] * 6,
        )

    sent = second(tuple((h, k, a - count) for h, k, a in blocks if a >= count), yt_near)
    yt_near, sent = lax.optimization_barrier((yt_near, sent))
    arrived = along_z(sent, count)
    sums = join(second(tuple(b for b in blocks if b[2] < count), yt_near), arrived)
    sums = lax.all_to_all(sums, "blk", 0, 0, axis_index_groups=quarters, tiled=True)
    new_target_potential = -0.5 * (log_sum(sums) - offset[0])
    return source_potential.reshape(per), new_target_potential


def solution(mesh):
    nz = ZRUN
    ny = mesh.shape["blk"] // nz
    nw = mesh.shape["wide"]
    placed = (
        P("blk", None),
        P("blk"),
        P(("wide", "blk"), None),
        P(("wide", "blk")),
        P(("wide", "blk")),
    )
    return jax.shard_map(
        functools.partial(per_device, nz, ny, nw),
        mesh=mesh,
        in_specs=placed,
        out_specs=(P("blk"), P(("wide", "blk"))),
        check_vma=False,
    )
```

```python
import functools

import jax
import jax.numpy as jnp
from jax import lax
from jax.experimental import pallas as pl
from jax.experimental.pallas import tpu as pltpu
from jax.sharding import PartitionSpec as P

ZRUN = 8
FEATURES = 64
EXTRA = 16
DEPTH = 128
ROWS = 512
LANES = 256
LOW = 2.0**-60
HIGH = 2.0**120


def three_parts(value):
    high = value.astype(jnp.bfloat16).astype(jnp.float32)
    rest = value - high
    middle = rest.astype(jnp.bfloat16).astype(jnp.float32)
    low = (rest - middle).astype(jnp.bfloat16).astype(jnp.float32)
    return high, middle, low


def extra_block(first, second):
    n = first[0].shape[1]
    row = lax.broadcasted_iota(jnp.int32, (EXTRA, n), 0)
    block = jnp.zeros((EXTRA, n), jnp.float32)
    for k, part in enumerate(tuple(first) + tuple(second)):
        block = jnp.where(row == k, part, block)
    return block


def ones_of(n):
    one = jnp.ones((1, n), jnp.float32)
    return one, one, one


def prepare_kernel(y_ref, logw_ref, potential_ref, out_ref, offset_ref):
    y = y_ref[...].astype(jnp.float32)
    offset = potential_ref[...] * 2.0 + logw_ref[...]
    bias = offset - jnp.sum(y * y, axis=0, keepdims=True)
    out_ref[0:FEATURES, :] = (y * 2.0).astype(jnp.bfloat16)
    out_ref[FEATURES : FEATURES + EXTRA, :] = extra_block(
        three_parts(bias), ones_of(bias.shape[1])
    ).astype(jnp.bfloat16)
    offset_ref[...] = offset


def copies_kernel(x_ref, out_ref, sem):
    moves = [
        pltpu.make_async_copy(x_ref, out_ref.at[k], sem.at[k]) for k in range(out_ref.shape[0])
    ]
    for move in moves:
        move.start()
    for move in moves:
        move.wait()


def weights_of(features, extra):
    rest = jnp.zeros((DEPTH - FEATURES - EXTRA, features.shape[1]), features.dtype)
    return jnp.concatenate([features, extra, rest], axis=0)


def product(a, b):
    return jnp.dot(a, b, preferred_element_type=jnp.float32)


def folded(value, combine):
    rows, n = value.shape
    return combine(value.reshape(rows // 8, 8, n), axis=0)


def join(a, b):
    top = jnp.maximum(a, b)
    return top + jnp.log(1.0 + jnp.exp(jnp.minimum(a, b) - top))


def first_kernel(last, *refs):
    y_ref, x_ref, refs = refs[0], refs[1], refs[2:]
    if last:
        before_ref, logw_ref, refs = refs[0], refs[1], refs[2:]
    yt_ref, l_ref, sums_ref = refs
    rows = yt_ref.shape[0]
    ny, _, per = x_ref.shape
    row_step = min(ROWS, rows)
    col_step = min(LANES, per)
    together = 2

    extra = y_ref[FEATURES : FEATURES + EXTRA, :].astype(jnp.float32)
    bias = extra[0:1, :] + extra[1:2, :] + extra[2:3, :]
    shift = jnp.max(bias, axis=1, keepdims=True)
    for k in range(0, rows, row_step):
        block = jnp.concatenate(
            [
                y_ref[:, k : k + row_step].astype(jnp.float32),
                jnp.zeros((DEPTH - FEATURES - EXTRA, row_step), jnp.float32),
            ],
            axis=0,
        )
        yt_ref[k : k + row_step, :] = block.T.astype(jnp.bfloat16)
    extra = extra_block(
        ones_of(col_step), three_parts(jnp.broadcast_to(-shift, (1, col_step)))
    ).astype(jnp.bfloat16)

    def store(row, value):
        if last:
            value = join(before_ref[row : row + 1, :], value)
        l_ref[row : row + 1, 0:per] = value

    if last:
        part = per // ny
        for k in range(ny):
            l_ref[k : k + 1, per:] = logw_ref[:, k * part : (k + 1) * part]

    def main(g, carry):
        for s in range(together):
            r = g * together + s
            for t in range(0, per, col_step):
                weights = weights_of(x_ref[r, :, t : t + col_step], extra)
                total = jnp.zeros((8, col_step), jnp.float32)
                for j in range(0, rows, row_step):
                    score = product(yt_ref[j : j + row_step, :], weights)
                    total = total + folded(jnp.exp(score), jnp.sum)
                sums_ref[r, :, t : t + col_step] = total
        return carry

    lax.fori_loop(0, ny // together, main, 0)
    total = jnp.sum(sums_ref[...], axis=1)
    result = shift + jnp.log(total)
    for r in range(ny):
        store(r, result[r : r + 1, :])

    @pl.when(jnp.logical_not((jnp.min(total) > LOW) & (jnp.max(total) < HIGH)))
    def _():
        def again(g, carry):
            at = pl.ds(pl.multiple_of(g * col_step, col_step), col_step)
            for r in range(ny):
                weights = weights_of(x_ref[r, :, at], extra)

                def advance(j, state):
                    top, total = state
                    here = pl.ds(pl.multiple_of(j * row_step, row_step), row_step)
                    score = product(yt_ref[here, :], weights)
                    new = jnp.maximum(top, jnp.max(score, axis=0, keepdims=True))
                    total = total * jnp.exp(top - new) + jnp.sum(
                        jnp.exp(score - new), axis=0, keepdims=True
                    )
                    return new, total

                start = (
                    jnp.full((1, col_step), -1e30, jnp.float32),
                    jnp.zeros((1, col_step), jnp.float32),
                )
                top, total = lax.fori_loop(0, rows // row_step, advance, start)
                sums_ref[r, 0:1, at] = shift + top + jnp.log(total)
            return carry

        lax.fori_loop(0, per // col_step, again, 0)
        for r in range(ny):
            store(r, sums_ref[r, 0:1, :])


def second_kernel(
    slots,
    place_ref,
    near_ref,
    far_ref,
    x_ref,
    total_ref,
    logw_ref,
    s_ref,
    extra_ref,
    left_ref,
    acc_ref,
    top_ref,
):
    nz, each = s_ref.shape
    rows = nz * each
    ny, _, per = x_ref.shape
    row_step = min(ROWS, rows)
    col_step = min(LANES, per)

    for r in range(ny):
        logw = jnp.concatenate([logw_ref[r, k : k + 1, per:] for k in range(ny)], axis=1)
        c = logw - total_ref[r : r + 1, :]
        extra_ref[r] = extra_block(ones_of(per), three_parts(c)).astype(jnp.bfloat16)
    for g, (half, k, _) in enumerate(slots):
        ref = far_ref if half else near_ref
        left_ref[g * each : (g + 1) * each, :] = ref[k * each : (k + 1) * each, :]

    def lanes_folded(value, combine):
        out = value[:, 0:128]
        for k in range(1, value.shape[1] // 128):
            out = combine(out, value[:, k * 128 : (k + 1) * 128])
        return out

    def main(g, carry):
        here = pl.ds(pl.multiple_of(g * row_step, row_step), row_step)
        left = left_ref[here, :]
        for r in range(ny):
            for t in range(0, per, col_step):
                at = slice(t, t + col_step)
                score = product(left, weights_of(x_ref[r, :, at], extra_ref[r, :, at]))
                part = lanes_folded(jnp.exp(score), jnp.add)
                if r == 0 and t == 0:
                    acc_ref[here, :] = part
                else:
                    acc_ref[here, :] = acc_ref[here, :] + part
        return carry

    lax.fori_loop(0, rows // row_step, main, 0)

    def store(result):
        for g, (_, _, row) in enumerate(slots):
            s_ref[pl.ds(place_ref[0] ^ row, 1), :] = result[:, g * each : (g + 1) * each]

    total = jnp.sum(acc_ref[...].T, axis=0, keepdims=True)
    store(jnp.log(total))

    @pl.when(jnp.logical_not((jnp.min(total) > LOW) & (jnp.max(total) < HIGH)))
    def _():
        def again(g, carry):
            here = pl.ds(pl.multiple_of(g * each, each), each)
            left = left_ref[here, :]
            state = (
                jnp.full((each, 128), -1e30, jnp.float32),
                jnp.zeros((each, 128), jnp.float32),
            )
            for r in range(ny):

                def advance(t, state):
                    top, total = state
                    at = pl.ds(pl.multiple_of(t * col_step, col_step), col_step)
                    score = product(left, weights_of(x_ref[r, :, at], extra_ref[r, :, at]))
                    new = jnp.maximum(top, lanes_folded(score, jnp.maximum))
                    total = total * jnp.exp(top - new)
                    for k in range(col_step // 128):
                        total = total + jnp.exp(score[:, k * 128 : (k + 1) * 128] - new)
                    return new, total

                state = lax.fori_loop(0, per // col_step, advance, state)
            top_ref[here, :] = state[0]
            acc_ref[here, :] = state[1]
            return carry

        lax.fori_loop(0, rows // each, again, 0)
        tops = top_ref[...].T
        top = jnp.max(tops, axis=0, keepdims=True)
        total = jnp.sum(acc_ref[...].T * jnp.exp(tops - top), axis=0, keepdims=True)
        store(top + jnp.log(total))


def call(kernel, outs, scratch, flops, exps, *args, spaces=None, out=None, limit=40):
    return pl.pallas_call(
        kernel,
        out_shape=outs,
        in_specs=[
            pl.BlockSpec(memory_space=space) for space in spaces or [pltpu.VMEM] * len(args)
        ],
        out_specs=jax.tree.map(lambda _: pl.BlockSpec(memory_space=out or pltpu.VMEM), outs),
        scratch_shapes=scratch,
        compiler_params=pltpu.CompilerParams(vmem_limit_bytes=limit * 2**20),
        cost_estimate=pl.CostEstimate(
            flops=flops, bytes_accessed=4 * 2**20, transcendentals=exps
        ),
    )(*args)


def log_sum(parts):
    top = jnp.max(parts, axis=0)
    return top + jnp.log(jnp.sum(jnp.exp(parts - top), axis=0))


def per_device(nz, ny, nw, source_latent, source_logw, target_latent, target_logw, target_potential):
    f32, bf16 = jnp.float32, jnp.bfloat16
    per = source_latent.shape[0]
    each = target_latent.shape[0]
    cols, half = ny * per, nz // 2 * each
    pairs = cols * half
    place = lax.axis_index("blk")
    my_y, my_z = place // nz, place % nz
    depth = FEATURES + EXTRA
    y_groups = [[y * nz + z for y in range(ny)] for z in range(nz)]
    quarters = [[g * (nz // 2) + z for z in range(nz // 2)] for g in range(2 * ny)]
    x_groups = [[h * (nw // 2) + k for k in range(nw // 2)] for h in range(2)]

    def along_z(value, k):
        perm = [(y * nz + z, y * nz + (z ^ k)) for y in range(ny) for z in range(nz)]
        return lax.ppermute(value, "blk", perm)

    def along_wide(value, k):
        return lax.ppermute(value, "wide", [(w, w ^ k) for w in range(nw)])

    def shared(value, axis, groups):
        spread = jnp.broadcast_to(value[None], (len(groups[0]),) + value.shape)
        return lax.all_to_all(spread, axis, 0, 0, axis_index_groups=groups, tiled=True)

    y, offset = call(
        prepare_kernel,
        (jax.ShapeDtypeStruct((depth, each), bf16), jax.ShapeDtypeStruct((1, each), f32)),
        [],
        each * FEATURES * 4,
        0,
        target_latent.T,
        target_logw.reshape(1, each),
        target_potential.reshape(1, each),
    )
    x = source_latent.T
    copies = call(
        copies_kernel,
        jax.ShapeDtypeStruct((ny, FEATURES, per), bf16),
        [pltpu.SemaphoreType.DMA((ny,))],
        0,
        0,
        x,
        spaces=[pl.ANY],
        out=pl.ANY,
        limit=60,
    )
    xs = lax.all_to_all(copies, "blk", 0, 0, axis_index_groups=y_groups, tiled=True)
    bit = nz // 2
    while bit > 1:
        y = jnp.concatenate([y, along_z(y, bit)], axis=1)
        bit //= 2
    far = along_z(y, 1)

    def first(block, *more):
        last = len(more) > 0
        return call(
            functools.partial(first_kernel, last),
            (
                jax.ShapeDtypeStruct((half, DEPTH), bf16),
                jax.ShapeDtypeStruct((ny, per + per // ny if last else per), f32),
            ),
            [pltpu.VMEM((ny, 8, per), f32)],
            2 * pairs * DEPTH,
            pairs,
            block,
            xs,
            *more,
        )

    yt_near, total = first(y)
    yt_far, total = first(far, total, source_logw.reshape(1, per))
    got = shared(total, "blk", y_groups)
    total = log_sum(got[:, :, :per])
    total = log_sum(shared(total, "wide", x_groups))
    total = join(total, along_wide(total, nw // 2))
    sq = jnp.sum(jnp.square(x.astype(f32)), axis=0, keepdims=True)
    mine = lax.dynamic_slice(total, (my_y, 0), (1, per))
    source_potential = -0.5 * (mine - sq)

    count = nz // 2
    width = count.bit_length() - 1
    blocks = []
    for h in range(2):
        for k in range(count):
            blocks.append((h, k, 2 * int(format(k, "b").zfill(width)[::-1], 2) + h))
    place_in = (my_z % count).astype(jnp.int32).reshape(1)

    def second(slots, near):
        return call(
            functools.partial(second_kernel, slots),
            jax.ShapeDtypeStruct((count, each), f32),
            [
                pltpu.VMEM((ny, EXTRA, per), bf16),
                pltpu.VMEM((half, DEPTH), bf16),
                pltpu.VMEM((half, 128), f32),
                pltpu.VMEM((half, 128), f32),
            ],
            2 * pairs * DEPTH,
            pairs,
            place_in,
            near,
            yt_far,
            xs,
            total,
            got,
            spaces=[pltpu.SMEM] + [pltpu.VMEM] * 5,
        )

    sent = second(tuple((h, k, a - count) for h, k, a in blocks if a >= count), yt_near)
    yt_near, sent = lax.optimization_barrier((yt_near, sent))
    arrived = along_z(sent, count)
    sums = join(second(tuple(b for b in blocks if b[2] < count), yt_near), arrived)
    sums = lax.all_to_all(sums, "blk", 0, 0, axis_index_groups=quarters, tiled=True)
    new_target_potential = -0.5 * (log_sum(sums) - offset[0])
    return source_potential.reshape(per), new_target_potential


def solution(mesh):
    nz = ZRUN
    ny = mesh.shape["blk"] // nz
    nw = mesh.shape["wide"]
    placed = (
        P("blk", None),
        P("blk"),
        P(("wide", "blk"), None),
        P(("wide", "blk")),
        P(("wide", "blk")),
    )
    return jax.shard_map(
        functools.partial(per_device, nz, ny, nw),
        mesh=mesh,
        in_specs=placed,
        out_specs=(P("blk"), P(("wide", "blk"))),
        check_vma=False,
    )
```

```python
import functools

import jax
import jax.numpy as jnp
from jax import lax
from jax.experimental import pallas as pl
from jax.experimental.pallas import tpu as pltpu
from jax.sharding import PartitionSpec as P

ZRUN = 8
FEATURES = 64
EXTRA = 16
DEPTH = 128
ROWS = 512
LANES = 256
LOW = 2.0**-60
HIGH = 2.0**120


def three_parts(value):
    high = value.astype(jnp.bfloat16).astype(jnp.float32)
    rest = value - high
    middle = rest.astype(jnp.bfloat16).astype(jnp.float32)
    low = (rest - middle).astype(jnp.bfloat16).astype(jnp.float32)
    return high, middle, low


def extra_block(first, second):
    n = first[0].shape[1]
    row = lax.broadcasted_iota(jnp.int32, (EXTRA, n), 0)
    block = jnp.zeros((EXTRA, n), jnp.float32)
    for k, part in enumerate(tuple(first) + tuple(second)):
        block = jnp.where(row == k, part, block)
    return block


def ones_of(n):
    one = jnp.ones((1, n), jnp.float32)
    return one, one, one


def prepare_kernel(
    x_in, y_in, logw_in, potential_in, out_ref, offset_ref, copies_ref, x_ref, y_ref, logw_ref, potential_ref, sem
):
    count = copies_ref.shape[0]
    pairs = [(x_in, x_ref), (y_in, y_ref), (logw_in, logw_ref), (potential_in, potential_ref)]
    pairs += [(x_ref, copies_ref.at[k]) for k in range(count)]
    moves = [
        pltpu.make_async_copy(source, target, sem.at[k])
        for k, (source, target) in enumerate(pairs)
    ]
    for move in moves[:4]:
        move.start()
    moves[0].wait()
    for move in moves[4:]:
        move.start()
    for move in moves[1:4]:
        move.wait()
    y = y_ref[...].astype(jnp.float32)
    offset = potential_ref[...] * 2.0 + logw_ref[...]
    bias = offset - jnp.sum(y * y, axis=0, keepdims=True)
    out_ref[0:FEATURES, :] = (y * 2.0).astype(jnp.bfloat16)
    out_ref[FEATURES : FEATURES + EXTRA, :] = extra_block(
        three_parts(bias), ones_of(bias.shape[1])
    ).astype(jnp.bfloat16)
    offset_ref[...] = offset
    for move in moves[4:]:
        move.wait()


def weights_of(features, extra):
    rest = jnp.zeros((DEPTH - FEATURES - EXTRA, features.shape[1]), features.dtype)
    return jnp.concatenate([features, extra, rest], axis=0)


def product(a, b):
    return jnp.dot(a, b, preferred_element_type=jnp.float32)


def folded(value, combine):
    rows, n = value.shape
    return combine(value.reshape(rows // 8, 8, n), axis=0)


def join(a, b):
    top = jnp.maximum(a, b)
    return top + jnp.log(1.0 + jnp.exp(jnp.minimum(a, b) - top))


def first_kernel(last, *refs):
    y_ref, x_ref, refs = refs[0], refs[1], refs[2:]
    if last:
        before_ref, logw_ref, refs = refs[0], refs[1], refs[2:]
    yt_ref, l_ref, sums_ref = refs
    rows = yt_ref.shape[0]
    ny, _, per = x_ref.shape
    row_step = min(ROWS, rows)
    col_step = min(LANES, per)
    together = 2

    extra = y_ref[FEATURES : FEATURES + EXTRA, :].astype(jnp.float32)
    bias = extra[0:1, :] + extra[1:2, :] + extra[2:3, :]
    shift = jnp.max(bias, axis=1, keepdims=True)
    for k in range(0, rows, row_step):
        block = jnp.concatenate(
            [
                y_ref[:, k : k + row_step].astype(jnp.float32),
                jnp.zeros((DEPTH - FEATURES - EXTRA, row_step), jnp.float32),
            ],
            axis=0,
        )
        yt_ref[k : k + row_step, :] = block.T.astype(jnp.bfloat16)
    extra = extra_block(
        ones_of(col_step), three_parts(jnp.broadcast_to(-shift, (1, col_step)))
    ).astype(jnp.bfloat16)

    def store(row, value):
        if last:
            value = join(before_ref[row : row + 1, :], value)
        l_ref[row : row + 1, 0:per] = value

    if last:
        part = per // ny
        for k in range(ny):
            l_ref[k : k + 1, per:] = logw_ref[:, k * part : (k + 1) * part]

    def main(g, carry):
        for s in range(together):
            r = g * together + s
            for t in range(0, per, col_step):
                weights = weights_of(x_ref[r, :, t : t + col_step], extra)
                total = jnp.zeros((8, col_step), jnp.float32)
                for j in range(0, rows, row_step):
                    score = product(yt_ref[j : j + row_step, :], weights)
                    total = total + folded(jnp.exp(score), jnp.sum)
                sums_ref[r, :, t : t + col_step] = total
        return carry

    lax.fori_loop(0, ny // together, main, 0)
    total = jnp.sum(sums_ref[...], axis=1)
    result = shift + jnp.log(total)
    for r in range(ny):
        store(r, result[r : r + 1, :])

    @pl.when(jnp.logical_not((jnp.min(total) > LOW) & (jnp.max(total) < HIGH)))
    def _():
        def again(g, carry):
            at = pl.ds(pl.multiple_of(g * col_step, col_step), col_step)
            for r in range(ny):
                weights = weights_of(x_ref[r, :, at], extra)

                def advance(j, state):
                    top, total = state
                    here = pl.ds(pl.multiple_of(j * row_step, row_step), row_step)
                    score = product(yt_ref[here, :], weights)
                    new = jnp.maximum(top, jnp.max(score, axis=0, keepdims=True))
                    total = total * jnp.exp(top - new) + jnp.sum(
                        jnp.exp(score - new), axis=0, keepdims=True
                    )
                    return new, total

                start = (
                    jnp.full((1, col_step), -1e30, jnp.float32),
                    jnp.zeros((1, col_step), jnp.float32),
                )
                top, total = lax.fori_loop(0, rows // row_step, advance, start)
                sums_ref[r, 0:1, at] = shift + top + jnp.log(total)
            return carry

        lax.fori_loop(0, per // col_step, again, 0)
        for r in range(ny):
            store(r, sums_ref[r, 0:1, :])


def second_kernel(
    slots,
    place_ref,
    near_ref,
    far_ref,
    x_ref,
    total_ref,
    logw_ref,
    s_ref,
    extra_ref,
    left_ref,
    acc_ref,
    top_ref,
):
    nz, each = s_ref.shape
    rows = nz * each
    ny, _, per = x_ref.shape
    row_step = min(ROWS, rows)
    col_step = min(LANES, per)

    for r in range(ny):
        logw = jnp.concatenate([logw_ref[r, k : k + 1, per:] for k in range(ny)], axis=1)
        c = logw - total_ref[r : r + 1, :]
        extra_ref[r] = extra_block(ones_of(per), three_parts(c)).astype(jnp.bfloat16)
    for g, (half, k, _) in enumerate(slots):
        ref = far_ref if half else near_ref
        left_ref[g * each : (g + 1) * each, :] = ref[k * each : (k + 1) * each, :]

    def lanes_folded(value, combine):
        out = value[:, 0:128]
        for k in range(1, value.shape[1] // 128):
            out = combine(out, value[:, k * 128 : (k + 1) * 128])
        return out

    def main(g, carry):
        here = pl.ds(pl.multiple_of(g * row_step, row_step), row_step)
        left = left_ref[here, :]
        for r in range(ny):
            for t in range(0, per, col_step):
                at = slice(t, t + col_step)
                score = product(left, weights_of(x_ref[r, :, at], extra_ref[r, :, at]))
                part = lanes_folded(jnp.exp(score), jnp.add)
                if r == 0 and t == 0:
                    acc_ref[here, :] = part
                else:
                    acc_ref[here, :] = acc_ref[here, :] + part
        return carry

    lax.fori_loop(0, rows // row_step, main, 0)

    def store(result):
        for g, (_, _, row) in enumerate(slots):
            s_ref[pl.ds(place_ref[0] ^ row, 1), :] = result[:, g * each : (g + 1) * each]

    total = jnp.sum(acc_ref[...].T, axis=0, keepdims=True)
    store(jnp.log(total))

    @pl.when(jnp.logical_not((jnp.min(total) > LOW) & (jnp.max(total) < HIGH)))
    def _():
        def again(g, carry):
            here = pl.ds(pl.multiple_of(g * each, each), each)
            left = left_ref[here, :]
            state = (
                jnp.full((each, 128), -1e30, jnp.float32),
                jnp.zeros((each, 128), jnp.float32),
            )
            for r in range(ny):

                def advance(t, state):
                    top, total = state
                    at = pl.ds(pl.multiple_of(t * col_step, col_step), col_step)
                    score = product(left, weights_of(x_ref[r, :, at], extra_ref[r, :, at]))
                    new = jnp.maximum(top, lanes_folded(score, jnp.maximum))
                    total = total * jnp.exp(top - new)
                    for k in range(col_step // 128):
                        total = total + jnp.exp(score[:, k * 128 : (k + 1) * 128] - new)
                    return new, total

                state = lax.fori_loop(0, per // col_step, advance, state)
            top_ref[here, :] = state[0]
            acc_ref[here, :] = state[1]
            return carry

        lax.fori_loop(0, rows // each, again, 0)
        tops = top_ref[...].T
        top = jnp.max(tops, axis=0, keepdims=True)
        total = jnp.sum(acc_ref[...].T * jnp.exp(tops - top), axis=0, keepdims=True)
        store(top + jnp.log(total))


def call(kernel, outs, scratch, flops, exps, *args, spaces=None, out=None, limit=40):
    out = out or jax.tree.map(lambda _: pltpu.VMEM, outs)
    return pl.pallas_call(
        kernel,
        out_shape=outs,
        in_specs=[
            pl.BlockSpec(memory_space=space) for space in spaces or [pltpu.VMEM] * len(args)
        ],
        out_specs=jax.tree.map(lambda space: pl.BlockSpec(memory_space=space), out),
        scratch_shapes=scratch,
        compiler_params=pltpu.CompilerParams(vmem_limit_bytes=limit * 2**20),
        cost_estimate=pl.CostEstimate(
            flops=flops, bytes_accessed=4 * 2**20, transcendentals=exps
        ),
    )(*args)


def log_sum(parts):
    top = jnp.max(parts, axis=0)
    return top + jnp.log(jnp.sum(jnp.exp(parts - top), axis=0))


def per_device(nz, ny, nw, source_latent, source_logw, target_latent, target_logw, target_potential):
    f32, bf16 = jnp.float32, jnp.bfloat16
    per = source_latent.shape[0]
    each = target_latent.shape[0]
    cols, half = ny * per, nz // 2 * each
    pairs = cols * half
    place = lax.axis_index("blk")
    my_y, my_z = place // nz, place % nz
    depth = FEATURES + EXTRA
    y_groups = [[y * nz + z for y in range(ny)] for z in range(nz)]
    quarters = [[g * (nz // 2) + z for z in range(nz // 2)] for g in range(2 * ny)]
    x_groups = [[h * (nw // 2) + k for k in range(nw // 2)] for h in range(2)]

    def along_z(value, k):
        perm = [(y * nz + z, y * nz + (z ^ k)) for y in range(ny) for z in range(nz)]
        return lax.ppermute(value, "blk", perm)

    def along_wide(value, k):
        return lax.ppermute(value, "wide", [(w, w ^ k) for w in range(nw)])

    def shared(value, axis, groups):
        spread = jnp.broadcast_to(value[None], (len(groups[0]),) + value.shape)
        return lax.all_to_all(spread, axis, 0, 0, axis_index_groups=groups, tiled=True)

    x = source_latent.T
    y, offset, copies = call(
        prepare_kernel,
        (
            jax.ShapeDtypeStruct((depth, each), bf16),
            jax.ShapeDtypeStruct((1, each), f32),
            jax.ShapeDtypeStruct((ny, FEATURES, per), bf16),
        ),
        [
            pltpu.VMEM((FEATURES, per), bf16),
            pltpu.VMEM((FEATURES, each), bf16),
            pltpu.VMEM((1, each), f32),
            pltpu.VMEM((1, each), f32),
            pltpu.SemaphoreType.DMA((4 + ny,)),
        ],
        each * FEATURES * 4,
        0,
        x,
        target_latent.T,
        target_logw.reshape(1, each),
        target_potential.reshape(1, each),
        spaces=[pl.ANY] * 4,
        out=(pltpu.VMEM, pltpu.VMEM, pl.ANY),
        limit=60,
    )
    xs = lax.all_to_all(copies, "blk", 0, 0, axis_index_groups=y_groups, tiled=True)
    bit = nz // 2
    while bit > 1:
        y = jnp.concatenate([y, along_z(y, bit)], axis=1)
        bit //= 2
    far = along_z(y, 1)

    def first(block, *more):
        last = len(more) > 0
        return call(
            functools.partial(first_kernel, last),
            (
                jax.ShapeDtypeStruct((half, DEPTH), bf16),
                jax.ShapeDtypeStruct((ny, per + per // ny if last else per), f32),
            ),
            [pltpu.VMEM((ny, 8, per), f32)],
            2 * pairs * DEPTH,
            pairs,
            block,
            xs,
            *more,
        )

    yt_near, total = first(y)
    yt_far, total = first(far, total, source_logw.reshape(1, per))
    got = shared(total, "blk", y_groups)
    total = log_sum(got[:, :, :per])
    total = log_sum(shared(total, "wide", x_groups))
    total = join(total, along_wide(total, nw // 2))
    sq = jnp.sum(jnp.square(x.astype(f32)), axis=0, keepdims=True)
    mine = lax.dynamic_slice(total, (my_y, 0), (1, per))
    source_potential = -0.5 * (mine - sq)

    count = nz // 2
    width = count.bit_length() - 1
    blocks = []
    for h in range(2):
        for k in range(count):
            blocks.append((h, k, 2 * int(format(k, "b").zfill(width)[::-1], 2) + h))
    place_in = (my_z % count).astype(jnp.int32).reshape(1)

    def second(slots, near):
        return call(
            functools.partial(second_kernel, slots),
            jax.ShapeDtypeStruct((count, each), f32),
            [
                pltpu.VMEM((ny, EXTRA, per), bf16),
                pltpu.VMEM((half, DEPTH), bf16),
                pltpu.VMEM((half, 128), f32),
                pltpu.VMEM((half, 128), f32),
            ],
            2 * pairs * DEPTH,
            pairs,
            place_in,
            near,
            yt_far,
            xs,
            total,
            got,
            spaces=[pltpu.SMEM] + [pltpu.VMEM] * 5,
        )

    sent = second(tuple((h, k, a - count) for h, k, a in blocks if a >= count), yt_near)
    yt_near, sent = lax.optimization_barrier((yt_near, sent))
    arrived = along_z(sent, count)
    sums = join(second(tuple(b for b in blocks if b[2] < count), yt_near), arrived)
    sums = lax.all_to_all(sums, "blk", 0, 0, axis_index_groups=quarters, tiled=True)
    new_target_potential = -0.5 * (log_sum(sums) - offset[0])
    return source_potential.reshape(per), new_target_potential


def solution(mesh):
    nz = ZRUN
    ny = mesh.shape["blk"] // nz
    nw = mesh.shape["wide"]
    placed = (
        P("blk", None),
        P("blk"),
        P(("wide", "blk"), None),
        P(("wide", "blk")),
        P(("wide", "blk")),
    )
    return jax.shard_map(
        functools.partial(per_device, nz, ny, nw),
        mesh=mesh,
        in_specs=placed,
        out_specs=(P("blk"), P(("wide", "blk"))),
        check_vma=False,
    )
```

```python
import functools

import jax
import jax.numpy as jnp
from jax import lax
from jax.experimental import pallas as pl
from jax.experimental.pallas import tpu as pltpu
from jax.sharding import PartitionSpec as P

ZRUN = 8
FEATURES = 64
EXTRA = 16
DEPTH = 128
ROWS = 512
LANES = 256
LOW = 2.0**-60
HIGH = 2.0**120


def three_parts(value):
    high = value.astype(jnp.bfloat16).astype(jnp.float32)
    rest = value - high
    middle = rest.astype(jnp.bfloat16).astype(jnp.float32)
    low = (rest - middle).astype(jnp.bfloat16).astype(jnp.float32)
    return high, middle, low


def extra_block(first, second):
    n = first[0].shape[1]
    row = lax.broadcasted_iota(jnp.int32, (EXTRA, n), 0)
    block = jnp.zeros((EXTRA, n), jnp.float32)
    for k, part in enumerate(tuple(first) + tuple(second)):
        block = jnp.where(row == k, part, block)
    return block


def ones_of(n):
    one = jnp.ones((1, n), jnp.float32)
    return one, one, one


def prepare_kernel(
    x_in,
    y_in,
    logw_in,
    potential_in,
    out_ref,
    offset_ref,
    upper_ref,
    lower_ref,
    x_ref,
    y_ref,
    logw_ref,
    potential_ref,
    sem,
):
    count = upper_ref.shape[0]
    half = FEATURES // 2
    pairs = [(x_in, x_ref), (y_in, y_ref), (logw_in, logw_ref), (potential_in, potential_ref)]
    pairs += [(x_ref.at[0:half], upper_ref.at[k]) for k in range(count)]
    pairs += [(x_ref.at[half:FEATURES], lower_ref.at[k]) for k in range(count)]
    moves = [
        pltpu.make_async_copy(source, target, sem.at[k])
        for k, (source, target) in enumerate(pairs)
    ]
    for move in moves[:4]:
        move.start()
    moves[0].wait()
    for move in moves[4:]:
        move.start()
    for move in moves[1:4]:
        move.wait()
    y = y_ref[...].astype(jnp.float32)
    offset = potential_ref[...] * 2.0 + logw_ref[...]
    bias = offset - jnp.sum(y * y, axis=0, keepdims=True)
    out_ref[0:FEATURES, :] = (y * 2.0).astype(jnp.bfloat16)
    out_ref[FEATURES : FEATURES + EXTRA, :] = extra_block(
        three_parts(bias), ones_of(bias.shape[1])
    ).astype(jnp.bfloat16)
    offset_ref[...] = offset
    for move in moves[4:]:
        move.wait()


def weights_of(upper_ref, lower_ref, r, at, extra):
    rest = jnp.zeros((DEPTH - FEATURES - EXTRA, extra.shape[1]), extra.dtype)
    return jnp.concatenate([upper_ref[r, :, at], lower_ref[r, :, at], extra, rest], axis=0)


def product(a, b):
    return jnp.dot(a, b, preferred_element_type=jnp.float32)


def folded(value, combine):
    rows, n = value.shape
    return combine(value.reshape(rows // 8, 8, n), axis=0)


def join(a, b):
    top = jnp.maximum(a, b)
    return top + jnp.log(1.0 + jnp.exp(jnp.minimum(a, b) - top))


def first_kernel(last, *refs):
    y_ref, upper_ref, lower_ref, refs = refs[0], refs[1], refs[2], refs[3:]
    if last:
        before_ref, logw_ref, yt_ref, l_ref, sums_ref = refs
    else:
        offset_ref, yt_ref, l_ref, kept_ref, sums_ref = refs
        kept_ref[...] = offset_ref[...]
    rows = yt_ref.shape[0]
    ny, _, per = upper_ref.shape
    row_step = min(ROWS, rows)
    col_step = min(LANES, per)
    together = 2

    extra = y_ref[FEATURES : FEATURES + EXTRA, :].astype(jnp.float32)
    bias = extra[0:1, :] + extra[1:2, :] + extra[2:3, :]
    shift = jnp.max(bias, axis=1, keepdims=True)
    for k in range(0, rows, row_step):
        block = jnp.concatenate(
            [
                y_ref[:, k : k + row_step].astype(jnp.float32),
                jnp.zeros((DEPTH - FEATURES - EXTRA, row_step), jnp.float32),
            ],
            axis=0,
        )
        yt_ref[k : k + row_step, :] = block.T.astype(jnp.bfloat16)
    extra = extra_block(
        ones_of(col_step), three_parts(jnp.broadcast_to(-shift, (1, col_step)))
    ).astype(jnp.bfloat16)

    def store(row, value):
        if last:
            value = join(before_ref[row : row + 1, :], value)
        l_ref[row : row + 1, 0:per] = value

    if last:
        part = per // ny
        for k in range(ny):
            l_ref[k : k + 1, per:] = logw_ref[:, k * part : (k + 1) * part]

    def main(g, carry):
        for s in range(together):
            r = g * together + s
            for t in range(0, per, col_step):
                weights = weights_of(upper_ref, lower_ref, r, slice(t, t + col_step), extra)
                total = jnp.zeros((8, col_step), jnp.float32)
                for j in range(0, rows, row_step):
                    score = product(yt_ref[j : j + row_step, :], weights)
                    total = total + folded(jnp.exp(score), jnp.sum)
                sums_ref[r, :, t : t + col_step] = total
        return carry

    lax.fori_loop(0, ny // together, main, 0)
    total = jnp.sum(sums_ref[...], axis=1)
    result = shift + jnp.log(total)
    for r in range(ny):
        store(r, result[r : r + 1, :])

    @pl.when(jnp.logical_not((jnp.min(total) > LOW) & (jnp.max(total) < HIGH)))
    def _():
        def again(g, carry):
            at = pl.ds(pl.multiple_of(g * col_step, col_step), col_step)
            for r in range(ny):
                weights = weights_of(upper_ref, lower_ref, r, at, extra)

                def advance(j, state):
                    top, total = state
                    here = pl.ds(pl.multiple_of(j * row_step, row_step), row_step)
                    score = product(yt_ref[here, :], weights)
                    new = jnp.maximum(top, jnp.max(score, axis=0, keepdims=True))
                    total = total * jnp.exp(top - new) + jnp.sum(
                        jnp.exp(score - new), axis=0, keepdims=True
                    )
                    return new, total

                start = (
                    jnp.full((1, col_step), -1e30, jnp.float32),
                    jnp.zeros((1, col_step), jnp.float32),
                )
                top, total = lax.fori_loop(0, rows // row_step, advance, start)
                sums_ref[r, 0:1, at] = shift + top + jnp.log(total)
            return carry

        lax.fori_loop(0, per // col_step, again, 0)
        for r in range(ny):
            store(r, sums_ref[r, 0:1, :])


def second_kernel(
    slots,
    place_ref,
    near_ref,
    far_ref,
    upper_ref,
    lower_ref,
    total_ref,
    logw_ref,
    s_ref,
    extra_ref,
    left_ref,
    acc_ref,
    top_ref,
):
    nz, each = s_ref.shape
    rows = nz * each
    ny, _, per = upper_ref.shape
    row_step = min(ROWS, rows)
    col_step = min(LANES, per)

    for r in range(ny):
        logw = jnp.concatenate([logw_ref[r, k : k + 1, per:] for k in range(ny)], axis=1)
        c = logw - total_ref[r : r + 1, :]
        extra_ref[r] = extra_block(ones_of(per), three_parts(c)).astype(jnp.bfloat16)
    for g, (half, k, _) in enumerate(slots):
        ref = far_ref if half else near_ref
        left_ref[g * each : (g + 1) * each, :] = ref[k * each : (k + 1) * each, :]

    def lanes_folded(value, combine):
        out = value[:, 0:128]
        for k in range(1, value.shape[1] // 128):
            out = combine(out, value[:, k * 128 : (k + 1) * 128])
        return out

    def main(g, carry):
        here = pl.ds(pl.multiple_of(g * row_step, row_step), row_step)
        left = left_ref[here, :]
        for r in range(ny):
            for t in range(0, per, col_step):
                at = slice(t, t + col_step)
                score = product(left, weights_of(upper_ref, lower_ref, r, at, extra_ref[r, :, at]))
                part = lanes_folded(jnp.exp(score), jnp.add)
                if r == 0 and t == 0:
                    acc_ref[here, :] = part
                else:
                    acc_ref[here, :] = acc_ref[here, :] + part
        return carry

    lax.fori_loop(0, rows // row_step, main, 0)

    def store(result):
        for g, (_, _, row) in enumerate(slots):
            s_ref[pl.ds(place_ref[0] ^ row, 1), :] = result[:, g * each : (g + 1) * each]

    total = jnp.sum(acc_ref[...].T, axis=0, keepdims=True)
    store(jnp.log(total))

    @pl.when(jnp.logical_not((jnp.min(total) > LOW) & (jnp.max(total) < HIGH)))
    def _():
        def again(g, carry):
            here = pl.ds(pl.multiple_of(g * each, each), each)
            left = left_ref[here, :]
            state = (
                jnp.full((each, 128), -1e30, jnp.float32),
                jnp.zeros((each, 128), jnp.float32),
            )
            for r in range(ny):

                def advance(t, state):
                    top, total = state
                    at = pl.ds(pl.multiple_of(t * col_step, col_step), col_step)
                    score = product(left, weights_of(upper_ref, lower_ref, r, at, extra_ref[r, :, at]))
                    new = jnp.maximum(top, lanes_folded(score, jnp.maximum))
                    total = total * jnp.exp(top - new)
                    for k in range(col_step // 128):
                        total = total + jnp.exp(score[:, k * 128 : (k + 1) * 128] - new)
                    return new, total

                state = lax.fori_loop(0, per // col_step, advance, state)
            top_ref[here, :] = state[0]
            acc_ref[here, :] = state[1]
            return carry

        lax.fori_loop(0, rows // each, again, 0)
        tops = top_ref[...].T
        top = jnp.max(tops, axis=0, keepdims=True)
        total = jnp.sum(acc_ref[...].T * jnp.exp(tops - top), axis=0, keepdims=True)
        store(top + jnp.log(total))


def call(kernel, outs, scratch, flops, exps, *args, spaces=None, out=None, limit=40):
    out = out or jax.tree.map(lambda _: pltpu.VMEM, outs)
    return pl.pallas_call(
        kernel,
        out_shape=outs,
        in_specs=[
            pl.BlockSpec(memory_space=space) for space in spaces or [pltpu.VMEM] * len(args)
        ],
        out_specs=jax.tree.map(lambda space: pl.BlockSpec(memory_space=space), out),
        scratch_shapes=scratch,
        compiler_params=pltpu.CompilerParams(vmem_limit_bytes=limit * 2**20),
        cost_estimate=pl.CostEstimate(
            flops=flops, bytes_accessed=4 * 2**20, transcendentals=exps
        ),
    )(*args)


def log_sum(parts):
    top = jnp.max(parts, axis=0)
    return top + jnp.log(jnp.sum(jnp.exp(parts - top), axis=0))


def per_device(nz, ny, nw, source_latent, source_logw, target_latent, target_logw, target_potential):
    f32, bf16 = jnp.float32, jnp.bfloat16
    per = source_latent.shape[0]
    each = target_latent.shape[0]
    cols, half = ny * per, nz // 2 * each
    pairs = cols * half
    place = lax.axis_index("blk")
    my_y, my_z = place // nz, place % nz
    depth = FEATURES + EXTRA
    y_groups = [[y * nz + z for y in range(ny)] for z in range(nz)]
    quarters = [[g * (nz // 2) + z for z in range(nz // 2)] for g in range(2 * ny)]
    x_groups = [[h * (nw // 2) + k for k in range(nw // 2)] for h in range(2)]

    def along_z(value, k):
        perm = [(y * nz + z, y * nz + (z ^ k)) for y in range(ny) for z in range(nz)]
        return lax.ppermute(value, "blk", perm)

    def along_wide(value, k):
        return lax.ppermute(value, "wide", [(w, w ^ k) for w in range(nw)])

    def shared(value, axis, groups):
        spread = jnp.broadcast_to(value[None], (len(groups[0]),) + value.shape)
        return lax.all_to_all(spread, axis, 0, 0, axis_index_groups=groups, tiled=True)

    x = source_latent.T
    y, offset, *copies = call(
        prepare_kernel,
        (
            jax.ShapeDtypeStruct((depth, each), bf16),
            jax.ShapeDtypeStruct((1, each), f32),
            jax.ShapeDtypeStruct((ny, FEATURES // 2, per), bf16),
            jax.ShapeDtypeStruct((ny, FEATURES // 2, per), bf16),
        ),
        [
            pltpu.VMEM((FEATURES, per), bf16),
            pltpu.VMEM((FEATURES, each), bf16),
            pltpu.VMEM((1, each), f32),
            pltpu.VMEM((1, each), f32),
            pltpu.SemaphoreType.DMA((4 + 2 * ny,)),
        ],
        each * FEATURES * 4,
        0,
        x,
        target_latent.T,
        target_logw.reshape(1, each),
        target_potential.reshape(1, each),
        spaces=[pl.ANY] * 4,
        out=(pltpu.VMEM, pltpu.VMEM, pl.ANY, pl.ANY),
        limit=60,
    )
    xs = [
        lax.all_to_all(part, "blk", 0, 0, axis_index_groups=y_groups, tiled=True) for part in copies
    ]
    bit = nz // 2
    while bit > 1:
        y = jnp.concatenate([y, along_z(y, bit)], axis=1)
        bit //= 2
    far = along_z(y, 1)

    def first(block, *more):
        last = len(more) > 1
        return call(
            functools.partial(first_kernel, last),
            (
                jax.ShapeDtypeStruct((half, DEPTH), bf16),
                jax.ShapeDtypeStruct((ny, per + per // ny if last else per), f32),
            )
            + (() if last else (jax.ShapeDtypeStruct((1, each), f32),)),
            [pltpu.VMEM((ny, 8, per), f32)],
            2 * pairs * DEPTH,
            pairs,
            block,
            *xs,
            *more,
        )

    yt_near, total, offset = first(y, offset)
    yt_far, total = first(far, total, source_logw.reshape(1, per))
    got = shared(total, "blk", y_groups)
    total = log_sum(got[:, :, :per])
    total = log_sum(shared(total, "wide", x_groups))
    total = join(total, along_wide(total, nw // 2))
    sq = jnp.sum(jnp.square(x.astype(f32)), axis=0, keepdims=True)
    mine = lax.dynamic_slice(total, (my_y, 0), (1, per))
    source_potential = -0.5 * (mine - sq)

    count = nz // 2
    width = count.bit_length() - 1
    blocks = []
    for h in range(2):
        for k in range(count):
            blocks.append((h, k, 2 * int(format(k, "b").zfill(width)[::-1], 2) + h))
    place_in = (my_z % count).astype(jnp.int32).reshape(1)

    def second(slots, near):
        return call(
            functools.partial(second_kernel, slots),
            jax.ShapeDtypeStruct((count, each), f32),
            [
                pltpu.VMEM((ny, EXTRA, per), bf16),
                pltpu.VMEM((half, DEPTH), bf16),
                pltpu.VMEM((half, 128), f32),
                pltpu.VMEM((half, 128), f32),
            ],
            2 * pairs * DEPTH,
            pairs,
            place_in,
            near,
            yt_far,
            *xs,
            total,
            got,
            spaces=[pltpu.SMEM] + [pltpu.VMEM] * 6,
        )

    sent = second(tuple((h, k, a - count) for h, k, a in blocks if a >= count), yt_near)
    yt_near, sent = lax.optimization_barrier((yt_near, sent))
    arrived = along_z(sent, count)
    sums = join(second(tuple(b for b in blocks if b[2] < count), yt_near), arrived)
    sums = lax.all_to_all(sums, "blk", 0, 0, axis_index_groups=quarters, tiled=True)
    new_target_potential = -0.5 * (log_sum(sums) - offset[0])
    return source_potential.reshape(per), new_target_potential


def solution(mesh):
    nz = ZRUN
    ny = mesh.shape["blk"] // nz
    nw = mesh.shape["wide"]
    placed = (
        P("blk", None),
        P("blk"),
        P(("wide", "blk"), None),
        P(("wide", "blk")),
        P(("wide", "blk")),
    )
    return jax.shard_map(
        functools.partial(per_device, nz, ny, nw),
        mesh=mesh,
        in_specs=placed,
        out_specs=(P("blk"), P(("wide", "blk"))),
        check_vma=False,
    )
```

```python
import functools

import jax
import jax.numpy as jnp
from jax import lax
from jax.experimental import pallas as pl
from jax.experimental.pallas import tpu as pltpu
from jax.sharding import PartitionSpec as P

ZRUN = 8
FEATURES = 64
EXTRA = 16
DEPTH = 128
ROWS = 512
LANES = 256
LOW = 2.0**-60
HIGH = 2.0**120


def three_parts(value):
    high = value.astype(jnp.bfloat16).astype(jnp.float32)
    rest = value - high
    middle = rest.astype(jnp.bfloat16).astype(jnp.float32)
    low = (rest - middle).astype(jnp.bfloat16).astype(jnp.float32)
    return high, middle, low


def extra_block(first, second):
    n = first[0].shape[1]
    row = lax.broadcasted_iota(jnp.int32, (EXTRA, n), 0)
    block = jnp.zeros((EXTRA, n), jnp.float32)
    for k, part in enumerate(tuple(first) + tuple(second)):
        block = jnp.where(row == k, part, block)
    return block


def ones_of(n):
    one = jnp.ones((1, n), jnp.float32)
    return one, one, one


def prepare_kernel(
    x_in, y_in, logw_in, potential_in, out_ref, offset_ref, copies_ref, x_ref, y_ref, logw_ref, potential_ref, sem
):
    count = copies_ref.shape[0]
    pairs = [(x_in, x_ref), (y_in, y_ref), (logw_in, logw_ref), (potential_in, potential_ref)]
    pairs += [(x_ref, copies_ref.at[k]) for k in range(count)]
    moves = [
        pltpu.make_async_copy(source, target, sem.at[k])
        for k, (source, target) in enumerate(pairs)
    ]
    for move in moves[:4]:
        move.start()
    moves[0].wait()
    for move in moves[4:]:
        move.start()
    for move in moves[1:4]:
        move.wait()
    y = y_ref[...].astype(jnp.float32)
    offset = potential_ref[...] * 2.0 + logw_ref[...]
    bias = offset - jnp.sum(y * y, axis=0, keepdims=True)
    out_ref[0:FEATURES, :] = (y * 2.0).astype(jnp.bfloat16)
    out_ref[FEATURES : FEATURES + EXTRA, :] = extra_block(
        three_parts(bias), ones_of(bias.shape[1])
    ).astype(jnp.bfloat16)
    offset_ref[...] = offset
    for move in moves[4:]:
        move.wait()


def weights_of(features, extra):
    rest = jnp.zeros((DEPTH - FEATURES - EXTRA, features.shape[1]), features.dtype)
    return jnp.concatenate([features, extra, rest], axis=0)


def product(a, b):
    return jnp.dot(a, b, preferred_element_type=jnp.float32)


def folded(value, combine):
    rows, n = value.shape
    return combine(value.reshape(rows // 8, 8, n), axis=0)


def join(a, b):
    top = jnp.maximum(a, b)
    return top + jnp.log(1.0 + jnp.exp(jnp.minimum(a, b) - top))


def turn_kernel(y_ref, yt_ref):
    rows = yt_ref.shape[0]
    row_step = min(ROWS, rows)
    for k in range(0, rows, row_step):
        block = jnp.concatenate(
            [
                y_ref[:, k : k + row_step].astype(jnp.float32),
                jnp.zeros((DEPTH - FEATURES - EXTRA, row_step), jnp.float32),
            ],
            axis=0,
        )
        yt_ref[k : k + row_step, :] = block.T.astype(jnp.bfloat16)


def first_kernel(last, *refs):
    y_ref, x_ref, refs = refs[0], refs[1], refs[2:]
    if last:
        before_ref, logw_ref, yt_ref, l_ref, sums_ref = refs
        turn_kernel(y_ref, yt_ref)
    else:
        offset_ref, yt_ref, l_ref, kept_ref, sums_ref = refs
        kept_ref[...] = offset_ref[...]
    rows = yt_ref.shape[0]
    ny, _, per = x_ref.shape
    row_step = min(ROWS, rows)
    col_step = min(LANES, per)
    together = 2

    extra = y_ref[FEATURES : FEATURES + EXTRA, :].astype(jnp.float32)
    bias = extra[0:1, :] + extra[1:2, :] + extra[2:3, :]
    shift = jnp.max(bias, axis=1, keepdims=True)
    extra = extra_block(
        ones_of(col_step), three_parts(jnp.broadcast_to(-shift, (1, col_step)))
    ).astype(jnp.bfloat16)

    def store(row, value):
        if last:
            value = join(before_ref[row : row + 1, :], value)
        l_ref[row : row + 1, 0:per] = value

    if last:
        part = per // ny
        for k in range(ny):
            l_ref[k : k + 1, per:] = logw_ref[:, k * part : (k + 1) * part]

    def main(g, carry):
        for s in range(together):
            r = g * together + s
            for t in range(0, per, col_step):
                weights = weights_of(x_ref[r, :, t : t + col_step], extra)
                total = jnp.zeros((8, col_step), jnp.float32)
                for j in range(0, rows, row_step):
                    score = product(yt_ref[j : j + row_step, :], weights)
                    total = total + folded(jnp.exp(score), jnp.sum)
                sums_ref[r, :, t : t + col_step] = total
        return carry

    lax.fori_loop(0, ny // together, main, 0)
    total = jnp.sum(sums_ref[...], axis=1)
    result = shift + jnp.log(total)
    for r in range(ny):
        store(r, result[r : r + 1, :])

    @pl.when(jnp.logical_not((jnp.min(total) > LOW) & (jnp.max(total) < HIGH)))
    def _():
        def again(g, carry):
            at = pl.ds(pl.multiple_of(g * col_step, col_step), col_step)
            for r in range(ny):
                weights = weights_of(x_ref[r, :, at], extra)

                def advance(j, state):
                    top, total = state
                    here = pl.ds(pl.multiple_of(j * row_step, row_step), row_step)
                    score = product(yt_ref[here, :], weights)
                    new = jnp.maximum(top, jnp.max(score, axis=0, keepdims=True))
                    total = total * jnp.exp(top - new) + jnp.sum(
                        jnp.exp(score - new), axis=0, keepdims=True
                    )
                    return new, total

                start = (
                    jnp.full((1, col_step), -1e30, jnp.float32),
                    jnp.zeros((1, col_step), jnp.float32),
                )
                top, total = lax.fori_loop(0, rows // row_step, advance, start)
                sums_ref[r, 0:1, at] = shift + top + jnp.log(total)
            return carry

        lax.fori_loop(0, per // col_step, again, 0)
        for r in range(ny):
            store(r, sums_ref[r, 0:1, :])


def second_kernel(
    slots,
    place_ref,
    near_ref,
    far_ref,
    x_ref,
    total_ref,
    logw_ref,
    s_ref,
    extra_ref,
    left_ref,
    acc_ref,
    top_ref,
):
    nz, each = s_ref.shape
    rows = nz * each
    ny, _, per = x_ref.shape
    row_step = min(ROWS, rows)
    col_step = min(LANES, per)

    for r in range(ny):
        logw = jnp.concatenate([logw_ref[r, k : k + 1, per:] for k in range(ny)], axis=1)
        c = logw - total_ref[r : r + 1, :]
        extra_ref[r] = extra_block(ones_of(per), three_parts(c)).astype(jnp.bfloat16)
    for g, (half, k, _) in enumerate(slots):
        ref = far_ref if half else near_ref
        left_ref[g * each : (g + 1) * each, :] = ref[k * each : (k + 1) * each, :]

    def lanes_folded(value, combine):
        out = value[:, 0:128]
        for k in range(1, value.shape[1] // 128):
            out = combine(out, value[:, k * 128 : (k + 1) * 128])
        return out

    def main(g, carry):
        here = pl.ds(pl.multiple_of(g * row_step, row_step), row_step)
        left = left_ref[here, :]
        for r in range(ny):
            for t in range(0, per, col_step):
                at = slice(t, t + col_step)
                score = product(left, weights_of(x_ref[r, :, at], extra_ref[r, :, at]))
                part = lanes_folded(jnp.exp(score), jnp.add)
                if r == 0 and t == 0:
                    acc_ref[here, :] = part
                else:
                    acc_ref[here, :] = acc_ref[here, :] + part
        return carry

    lax.fori_loop(0, rows // row_step, main, 0)

    def store(result):
        for g, (_, _, row) in enumerate(slots):
            s_ref[pl.ds(place_ref[0] ^ row, 1), :] = result[:, g * each : (g + 1) * each]

    total = jnp.sum(acc_ref[...].T, axis=0, keepdims=True)
    store(jnp.log(total))

    @pl.when(jnp.logical_not((jnp.min(total) > LOW) & (jnp.max(total) < HIGH)))
    def _():
        def again(g, carry):
            here = pl.ds(pl.multiple_of(g * each, each), each)
            left = left_ref[here, :]
            state = (
                jnp.full((each, 128), -1e30, jnp.float32),
                jnp.zeros((each, 128), jnp.float32),
            )
            for r in range(ny):

                def advance(t, state):
                    top, total = state
                    at = pl.ds(pl.multiple_of(t * col_step, col_step), col_step)
                    score = product(left, weights_of(x_ref[r, :, at], extra_ref[r, :, at]))
                    new = jnp.maximum(top, lanes_folded(score, jnp.maximum))
                    total = total * jnp.exp(top - new)
                    for k in range(col_step // 128):
                        total = total + jnp.exp(score[:, k * 128 : (k + 1) * 128] - new)
                    return new, total

                state = lax.fori_loop(0, per // col_step, advance, state)
            top_ref[here, :] = state[0]
            acc_ref[here, :] = state[1]
            return carry

        lax.fori_loop(0, rows // each, again, 0)
        tops = top_ref[...].T
        top = jnp.max(tops, axis=0, keepdims=True)
        total = jnp.sum(acc_ref[...].T * jnp.exp(tops - top), axis=0, keepdims=True)
        store(top + jnp.log(total))


def call(
    kernel, outs, scratch, flops, exps, *args, spaces=None, out=None, limit=40, moved=4 * 2**20
):
    out = out or jax.tree.map(lambda _: pltpu.VMEM, outs)
    return pl.pallas_call(
        kernel,
        out_shape=outs,
        in_specs=[
            pl.BlockSpec(memory_space=space) for space in spaces or [pltpu.VMEM] * len(args)
        ],
        out_specs=jax.tree.map(lambda space: pl.BlockSpec(memory_space=space), out),
        scratch_shapes=scratch,
        compiler_params=pltpu.CompilerParams(vmem_limit_bytes=limit * 2**20),
        cost_estimate=pl.CostEstimate(
            flops=flops, bytes_accessed=moved, transcendentals=exps
        ),
    )(*args)


def log_sum(parts):
    top = jnp.max(parts, axis=0)
    return top + jnp.log(jnp.sum(jnp.exp(parts - top), axis=0))


def per_device(nz, ny, nw, source_latent, source_logw, target_latent, target_logw, target_potential):
    f32, bf16 = jnp.float32, jnp.bfloat16
    per = source_latent.shape[0]
    each = target_latent.shape[0]
    cols, half = ny * per, nz // 2 * each
    pairs = cols * half
    place = lax.axis_index("blk")
    my_y, my_z = place // nz, place % nz
    depth = FEATURES + EXTRA
    y_groups = [[y * nz + z for y in range(ny)] for z in range(nz)]
    quarters = [[g * (nz // 2) + z for z in range(nz // 2)] for g in range(2 * ny)]
    x_groups = [[h * (nw // 2) + k for k in range(nw // 2)] for h in range(2)]

    def along_z(value, k):
        perm = [(y * nz + z, y * nz + (z ^ k)) for y in range(ny) for z in range(nz)]
        return lax.ppermute(value, "blk", perm)

    def along_wide(value, k):
        return lax.ppermute(value, "wide", [(w, w ^ k) for w in range(nw)])

    def shared(value, axis, groups):
        spread = jnp.broadcast_to(value[None], (len(groups[0]),) + value.shape)
        return lax.all_to_all(spread, axis, 0, 0, axis_index_groups=groups, tiled=True)

    x = source_latent.T
    y, offset, copies = call(
        prepare_kernel,
        (
            jax.ShapeDtypeStruct((depth, each), bf16),
            jax.ShapeDtypeStruct((1, each), f32),
            jax.ShapeDtypeStruct((ny, FEATURES, per), bf16),
        ),
        [
            pltpu.VMEM((FEATURES, per), bf16),
            pltpu.VMEM((FEATURES, each), bf16),
            pltpu.VMEM((1, each), f32),
            pltpu.VMEM((1, each), f32),
            pltpu.SemaphoreType.DMA((4 + ny,)),
        ],
        each * FEATURES * 4,
        0,
        x,
        target_latent.T,
        target_logw.reshape(1, each),
        target_potential.reshape(1, each),
        spaces=[pl.ANY] * 4,
        out=(pltpu.VMEM, pltpu.VMEM, pl.ANY),
        limit=60,
    )
    xs = lax.all_to_all(copies, "blk", 0, 0, axis_index_groups=y_groups, tiled=True)
    bit = nz // 2
    while bit > 1:
        y = jnp.concatenate([y, along_z(y, bit)], axis=1)
        bit //= 2
    far = along_z(y, 1)

    def first(block, *more):
        last = len(more) == 2 and more[0].shape[0] == ny
        return call(
            functools.partial(first_kernel, last),
            (
                jax.ShapeDtypeStruct((half, DEPTH), bf16),
                jax.ShapeDtypeStruct((ny, per + per // ny), f32),
            )
            if last
            else (jax.ShapeDtypeStruct((ny, per), f32), jax.ShapeDtypeStruct((1, each), f32)),
            [pltpu.VMEM((ny, 8, per), f32)],
            2 * pairs * DEPTH,
            pairs,
            block,
            xs,
            *more,
        )

    yt_near = call(
        turn_kernel,
        jax.ShapeDtypeStruct((half, DEPTH), bf16),
        [],
        0,
        0,
        y,
        moved=11 * 10**6,
    )
    total, offset = first(y, offset, yt_near)
    yt_far, total = first(far, total, source_logw.reshape(1, per))
    got = shared(total, "blk", y_groups)
    total = log_sum(got[:, :, :per])
    total = log_sum(shared(total, "wide", x_groups))
    total = join(total, along_wide(total, nw // 2))
    sq = jnp.sum(jnp.square(x.astype(f32)), axis=0, keepdims=True)
    mine = lax.dynamic_slice(total, (my_y, 0), (1, per))
    source_potential = -0.5 * (mine - sq)

    count = nz // 2
    width = count.bit_length() - 1
    blocks = []
    for h in range(2):
        for k in range(count):
            blocks.append((h, k, 2 * int(format(k, "b").zfill(width)[::-1], 2) + h))
    place_in = (my_z % count).astype(jnp.int32).reshape(1)

    def second(slots, near):
        return call(
            functools.partial(second_kernel, slots),
            jax.ShapeDtypeStruct((count, each), f32),
            [
                pltpu.VMEM((ny, EXTRA, per), bf16),
                pltpu.VMEM((half, DEPTH), bf16),
                pltpu.VMEM((half, 128), f32),
                pltpu.VMEM((half, 128), f32),
            ],
            2 * pairs * DEPTH,
            pairs,
            place_in,
            near,
            yt_far,
            xs,
            total,
            got,
            spaces=[pltpu.SMEM] + [pltpu.VMEM] * 5,
        )

    sent = second(tuple((h, k, a - count) for h, k, a in blocks if a >= count), yt_near)
    yt_near, sent = lax.optimization_barrier((yt_near, sent))
    arrived = along_z(sent, count)
    sums = join(second(tuple(b for b in blocks if b[2] < count), yt_near), arrived)
    sums = lax.all_to_all(sums, "blk", 0, 0, axis_index_groups=quarters, tiled=True)
    new_target_potential = -0.5 * (log_sum(sums) - offset[0])
    return source_potential.reshape(per), new_target_potential


def solution(mesh):
    nz = ZRUN
    ny = mesh.shape["blk"] // nz
    nw = mesh.shape["wide"]
    placed = (
        P("blk", None),
        P("blk"),
        P(("wide", "blk"), None),
        P(("wide", "blk")),
        P(("wide", "blk")),
    )
    return jax.shard_map(
        functools.partial(per_device, nz, ny, nw),
        mesh=mesh,
        in_specs=placed,
        out_specs=(P("blk"), P(("wide", "blk"))),
        check_vma=False,
    )
```

```python
import functools

import jax
import jax.numpy as jnp
from jax import lax
from jax.experimental import pallas as pl
from jax.experimental.pallas import tpu as pltpu
from jax.sharding import PartitionSpec as P

ZRUN = 8
FEATURES = 64
EXTRA = 16
DEPTH = 128
ROWS = 512
LANES = 256
LOW = 2.0**-60
HIGH = 2.0**120


def three_parts(value):
    high = value.astype(jnp.bfloat16).astype(jnp.float32)
    rest = value - high
    middle = rest.astype(jnp.bfloat16).astype(jnp.float32)
    low = (rest - middle).astype(jnp.bfloat16).astype(jnp.float32)
    return high, middle, low


def extra_block(first, second):
    n = first[0].shape[1]
    row = lax.broadcasted_iota(jnp.int32, (EXTRA, n), 0)
    block = jnp.zeros((EXTRA, n), jnp.float32)
    for k, part in enumerate(tuple(first) + tuple(second)):
        block = jnp.where(row == k, part, block)
    return block


def ones_of(n):
    one = jnp.ones((1, n), jnp.float32)
    return one, one, one


def prepare_kernel(
    x_in, y_in, logw_in, potential_in, out_ref, copies_ref, x_ref, y_ref, logw_ref, potential_ref, sem
):
    count = copies_ref.shape[0]
    pairs = [(x_in, x_ref), (y_in, y_ref), (logw_in, logw_ref), (potential_in, potential_ref)]
    pairs += [(x_ref, copies_ref.at[k]) for k in range(count)]
    moves = [
        pltpu.make_async_copy(source, target, sem.at[k])
        for k, (source, target) in enumerate(pairs)
    ]
    for move in moves[:4]:
        move.start()
    moves[0].wait()
    for move in moves[4:]:
        move.start()
    for move in moves[1:4]:
        move.wait()
    y = y_ref[...].astype(jnp.float32)
    bias = potential_ref[...] * 2.0 + logw_ref[...] - jnp.sum(y * y, axis=0, keepdims=True)
    out_ref[0:FEATURES, :] = (y * 2.0).astype(jnp.bfloat16)
    out_ref[FEATURES : FEATURES + EXTRA, :] = extra_block(
        three_parts(bias), ones_of(bias.shape[1])
    ).astype(jnp.bfloat16)
    for move in moves[4:]:
        move.wait()


def weights_of(features, extra):
    rest = jnp.zeros((DEPTH - FEATURES - EXTRA, features.shape[1]), features.dtype)
    return jnp.concatenate([features, extra, rest], axis=0)


def product(a, b):
    return jnp.dot(a, b, preferred_element_type=jnp.float32)


def folded(value, combine):
    rows, n = value.shape
    return combine(value.reshape(rows // 8, 8, n), axis=0)


def join(a, b):
    top = jnp.maximum(a, b)
    return top + jnp.log(1.0 + jnp.exp(jnp.minimum(a, b) - top))


def turn_kernel(y_ref, yt_ref):
    rows = yt_ref.shape[0]
    row_step = min(ROWS, rows)
    for k in range(0, rows, row_step):
        block = jnp.concatenate(
            [
                y_ref[:, k : k + row_step].astype(jnp.float32),
                jnp.zeros((DEPTH - FEATURES - EXTRA, row_step), jnp.float32),
            ],
            axis=0,
        )
        yt_ref[k : k + row_step, :] = block.T.astype(jnp.bfloat16)


def first_kernel(last, *refs):
    y_ref, x_ref, refs = refs[0], refs[1], refs[2:]
    if last:
        before_ref, logw_ref, yt_ref, l_ref, sums_ref = refs
        turn_kernel(y_ref, yt_ref)
    else:
        yt_ref, l_ref, sums_ref = refs
    rows = yt_ref.shape[0]
    ny, _, per = x_ref.shape
    row_step = min(ROWS, rows)
    col_step = min(LANES, per)
    together = 2

    extra = y_ref[FEATURES : FEATURES + EXTRA, :].astype(jnp.float32)
    bias = extra[0:1, :] + extra[1:2, :] + extra[2:3, :]
    shift = jnp.max(bias, axis=1, keepdims=True)
    extra = extra_block(
        ones_of(col_step), three_parts(jnp.broadcast_to(-shift, (1, col_step)))
    ).astype(jnp.bfloat16)

    def store(row, value):
        if last:
            value = join(before_ref[row : row + 1, :], value)
        l_ref[row : row + 1, 0:per] = value

    if last:
        part = per // ny
        for k in range(ny):
            l_ref[k : k + 1, per:] = logw_ref[:, k * part : (k + 1) * part]

    def main(g, carry):
        for s in range(together):
            r = g * together + s
            for t in range(0, per, col_step):
                weights = weights_of(x_ref[r, :, t : t + col_step], extra)
                total = jnp.zeros((8, col_step), jnp.float32)
                for j in range(0, rows, row_step):
                    score = product(yt_ref[j : j + row_step, :], weights)
                    total = total + folded(jnp.exp(score), jnp.sum)
                sums_ref[r, :, t : t + col_step] = total
        return carry

    lax.fori_loop(0, ny // together, main, 0)
    total = jnp.sum(sums_ref[...], axis=1)
    result = shift + jnp.log(total)
    for r in range(ny):
        store(r, result[r : r + 1, :])

    @pl.when(jnp.logical_not((jnp.min(total) > LOW) & (jnp.max(total) < HIGH)))
    def _():
        def again(g, carry):
            at = pl.ds(pl.multiple_of(g * col_step, col_step), col_step)
            for r in range(ny):
                weights = weights_of(x_ref[r, :, at], extra)

                def advance(j, state):
                    top, total = state
                    here = pl.ds(pl.multiple_of(j * row_step, row_step), row_step)
                    score = product(yt_ref[here, :], weights)
                    new = jnp.maximum(top, jnp.max(score, axis=0, keepdims=True))
                    total = total * jnp.exp(top - new) + jnp.sum(
                        jnp.exp(score - new), axis=0, keepdims=True
                    )
                    return new, total

                start = (
                    jnp.full((1, col_step), -1e30, jnp.float32),
                    jnp.zeros((1, col_step), jnp.float32),
                )
                top, total = lax.fori_loop(0, rows // row_step, advance, start)
                sums_ref[r, 0:1, at] = shift + top + jnp.log(total)
            return carry

        lax.fori_loop(0, per // col_step, again, 0)
        for r in range(ny):
            store(r, sums_ref[r, 0:1, :])


def second_kernel(
    slots,
    place_ref,
    near_ref,
    far_ref,
    x_ref,
    total_ref,
    logw_ref,
    s_ref,
    extra_ref,
    left_ref,
    acc_ref,
    top_ref,
):
    nz, each = s_ref.shape
    rows = nz * each
    ny, _, per = x_ref.shape
    row_step = min(ROWS, rows)
    col_step = min(LANES, per)

    for r in range(ny):
        logw = jnp.concatenate([logw_ref[r, k : k + 1, per:] for k in range(ny)], axis=1)
        c = logw - total_ref[r : r + 1, :]
        extra_ref[r] = extra_block(ones_of(per), three_parts(c)).astype(jnp.bfloat16)
    for g, (half, k, _) in enumerate(slots):
        ref = far_ref if half else near_ref
        left_ref[g * each : (g + 1) * each, :] = ref[k * each : (k + 1) * each, :]

    def lanes_folded(value, combine):
        out = value[:, 0:128]
        for k in range(1, value.shape[1] // 128):
            out = combine(out, value[:, k * 128 : (k + 1) * 128])
        return out

    def main(g, carry):
        here = pl.ds(pl.multiple_of(g * row_step, row_step), row_step)
        left = left_ref[here, :]
        for r in range(ny):
            for t in range(0, per, col_step):
                at = slice(t, t + col_step)
                score = product(left, weights_of(x_ref[r, :, at], extra_ref[r, :, at]))
                part = lanes_folded(jnp.exp(score), jnp.add)
                if r == 0 and t == 0:
                    acc_ref[here, :] = part
                else:
                    acc_ref[here, :] = acc_ref[here, :] + part
        return carry

    lax.fori_loop(0, rows // row_step, main, 0)

    def store(result):
        for g, (_, _, row) in enumerate(slots):
            s_ref[pl.ds(place_ref[0] ^ row, 1), :] = result[:, g * each : (g + 1) * each]

    total = jnp.sum(acc_ref[...].T, axis=0, keepdims=True)
    store(jnp.log(total))

    @pl.when(jnp.logical_not((jnp.min(total) > LOW) & (jnp.max(total) < HIGH)))
    def _():
        def again(g, carry):
            here = pl.ds(pl.multiple_of(g * each, each), each)
            left = left_ref[here, :]
            state = (
                jnp.full((each, 128), -1e30, jnp.float32),
                jnp.zeros((each, 128), jnp.float32),
            )
            for r in range(ny):

                def advance(t, state):
                    top, total = state
                    at = pl.ds(pl.multiple_of(t * col_step, col_step), col_step)
                    score = product(left, weights_of(x_ref[r, :, at], extra_ref[r, :, at]))
                    new = jnp.maximum(top, lanes_folded(score, jnp.maximum))
                    total = total * jnp.exp(top - new)
                    for k in range(col_step // 128):
                        total = total + jnp.exp(score[:, k * 128 : (k + 1) * 128] - new)
                    return new, total

                state = lax.fori_loop(0, per // col_step, advance, state)
            top_ref[here, :] = state[0]
            acc_ref[here, :] = state[1]
            return carry

        lax.fori_loop(0, rows // each, again, 0)
        tops = top_ref[...].T
        top = jnp.max(tops, axis=0, keepdims=True)
        total = jnp.sum(acc_ref[...].T * jnp.exp(tops - top), axis=0, keepdims=True)
        store(top + jnp.log(total))


def call(
    kernel, outs, scratch, flops, exps, *args, spaces=None, out=None, limit=40, moved=4 * 2**20
):
    out = out or jax.tree.map(lambda _: pltpu.VMEM, outs)
    return pl.pallas_call(
        kernel,
        out_shape=outs,
        in_specs=[
            pl.BlockSpec(memory_space=space) for space in spaces or [pltpu.VMEM] * len(args)
        ],
        out_specs=jax.tree.map(lambda space: pl.BlockSpec(memory_space=space), out),
        scratch_shapes=scratch,
        compiler_params=pltpu.CompilerParams(vmem_limit_bytes=limit * 2**20),
        cost_estimate=pl.CostEstimate(
            flops=flops, bytes_accessed=moved, transcendentals=exps
        ),
    )(*args)


def log_sum(parts):
    top = jnp.max(parts, axis=0)
    return top + jnp.log(jnp.sum(jnp.exp(parts - top), axis=0))


def per_device(nz, ny, nw, source_latent, source_logw, target_latent, target_logw, target_potential):
    f32, bf16 = jnp.float32, jnp.bfloat16
    per = source_latent.shape[0]
    each = target_latent.shape[0]
    cols, half = ny * per, nz // 2 * each
    pairs = cols * half
    place = lax.axis_index("blk")
    my_y, my_z = place // nz, place % nz
    depth = FEATURES + EXTRA
    y_groups = [[y * nz + z for y in range(ny)] for z in range(nz)]
    quarters = [[g * (nz // 2) + z for z in range(nz // 2)] for g in range(2 * ny)]
    x_groups = [[h * (nw // 2) + k for k in range(nw // 2)] for h in range(2)]

    def along_z(value, k):
        perm = [(y * nz + z, y * nz + (z ^ k)) for y in range(ny) for z in range(nz)]
        return lax.ppermute(value, "blk", perm)

    def along_wide(value, k):
        return lax.ppermute(value, "wide", [(w, w ^ k) for w in range(nw)])

    def shared(value, axis, groups):
        spread = jnp.broadcast_to(value[None], (len(groups[0]),) + value.shape)
        return lax.all_to_all(spread, axis, 0, 0, axis_index_groups=groups, tiled=True)

    x = source_latent.T
    y, copies = call(
        prepare_kernel,
        (
            jax.ShapeDtypeStruct((depth, each), bf16),
            jax.ShapeDtypeStruct((ny, FEATURES, per), bf16),
        ),
        [
            pltpu.VMEM((FEATURES, per), bf16),
            pltpu.VMEM((FEATURES, each), bf16),
            pltpu.VMEM((1, each), f32),
            pltpu.VMEM((1, each), f32),
            pltpu.SemaphoreType.DMA((4 + ny,)),
        ],
        each * FEATURES * 4,
        0,
        x,
        target_latent.T,
        target_logw.reshape(1, each),
        target_potential.reshape(1, each),
        spaces=[pl.ANY] * 4,
        out=(pltpu.VMEM, pl.ANY),
        limit=60,
    )
    xs = lax.all_to_all(copies, "blk", 0, 0, axis_index_groups=y_groups, tiled=True)
    bit = nz // 2
    while bit > 1:
        y = jnp.concatenate([y, along_z(y, bit)], axis=1)
        bit //= 2
    far = along_z(y, 1)

    def first(block, *more):
        last = len(more) == 2
        return call(
            functools.partial(first_kernel, last),
            (
                jax.ShapeDtypeStruct((half, DEPTH), bf16),
                jax.ShapeDtypeStruct((ny, per + per // ny), f32),
            )
            if last
            else jax.ShapeDtypeStruct((ny, per), f32),
            [pltpu.VMEM((ny, 8, per), f32)],
            2 * pairs * DEPTH,
            pairs,
            block,
            xs,
            *more,
        )

    yt_near = call(
        turn_kernel,
        jax.ShapeDtypeStruct((half, DEPTH), bf16),
        [],
        0,
        0,
        y,
        moved=27 * 10**6,
    )
    total = first(y, yt_near)
    yt_far, total = first(far, total, source_logw.reshape(1, per))
    got = shared(total, "blk", y_groups)
    total = log_sum(got[:, :, :per])
    total = log_sum(shared(total, "wide", x_groups))
    potential, total = lax.optimization_barrier((target_potential, total))
    offset = lax.optimization_barrier(potential * 2.0 + target_logw)
    total = join(total, along_wide(total, nw // 2))
    sq = jnp.sum(jnp.square(x.astype(f32)), axis=0, keepdims=True)
    mine = lax.dynamic_slice(total, (my_y, 0), (1, per))
    source_potential = -0.5 * (mine - sq)

    count = nz // 2
    width = count.bit_length() - 1
    blocks = []
    for h in range(2):
        for k in range(count):
            blocks.append((h, k, 2 * int(format(k, "b").zfill(width)[::-1], 2) + h))
    place_in = (my_z % count).astype(jnp.int32).reshape(1)

    def second(slots, near):
        return call(
            functools.partial(second_kernel, slots),
            jax.ShapeDtypeStruct((count, each), f32),
            [
                pltpu.VMEM((ny, EXTRA, per), bf16),
                pltpu.VMEM((half, DEPTH), bf16),
                pltpu.VMEM((half, 128), f32),
                pltpu.VMEM((half, 128), f32),
            ],
            2 * pairs * DEPTH,
            pairs,
            place_in,
            near,
            yt_far,
            xs,
            total,
            got,
            spaces=[pltpu.SMEM] + [pltpu.VMEM] * 5,
        )

    sent = second(tuple((h, k, a - count) for h, k, a in blocks if a >= count), yt_near)
    yt_near, sent = lax.optimization_barrier((yt_near, sent))
    arrived = along_z(sent, count)
    sums = join(second(tuple(b for b in blocks if b[2] < count), yt_near), arrived)
    sums = lax.all_to_all(sums, "blk", 0, 0, axis_index_groups=quarters, tiled=True)
    new_target_potential = -0.5 * (log_sum(sums) - offset)
    return source_potential.reshape(per), new_target_potential


def solution(mesh):
    nz = ZRUN
    ny = mesh.shape["blk"] // nz
    nw = mesh.shape["wide"]
    placed = (
        P("blk", None),
        P("blk"),
        P(("wide", "blk"), None),
        P(("wide", "blk")),
        P(("wide", "blk")),
    )
    return jax.shard_map(
        functools.partial(per_device, nz, ny, nw),
        mesh=mesh,
        in_specs=placed,
        out_specs=(P("blk"), P(("wide", "blk"))),
        check_vma=False,
    )
```

```python
import functools

import jax
import jax.numpy as jnp
from jax import lax
from jax.experimental import pallas as pl
from jax.experimental.pallas import tpu as pltpu
from jax.sharding import PartitionSpec as P

ZRUN = 8
FEATURES = 64
EXTRA = 16
DEPTH = 128
ROWS = 512
LANES = 256
LOW = 2.0**-60
HIGH = 2.0**120


def three_parts(value):
    high = value.astype(jnp.bfloat16).astype(jnp.float32)
    rest = value - high
    middle = rest.astype(jnp.bfloat16).astype(jnp.float32)
    low = (rest - middle).astype(jnp.bfloat16).astype(jnp.float32)
    return high, middle, low


def extra_block(first, second):
    n = first[0].shape[1]
    row = lax.broadcasted_iota(jnp.int32, (EXTRA, n), 0)
    block = jnp.zeros((EXTRA, n), jnp.float32)
    for k, part in enumerate(tuple(first) + tuple(second)):
        block = jnp.where(row == k, part, block)
    return block


def ones_of(n):
    one = jnp.ones((1, n), jnp.float32)
    return one, one, one


def prepare_kernel(
    x_in, y_in, logw_in, potential_in, out_ref, copies_ref, x_ref, y_ref, logw_ref, potential_ref, sem
):
    count = copies_ref.shape[0]
    pairs = [(x_in, x_ref), (y_in, y_ref), (logw_in, logw_ref), (potential_in, potential_ref)]
    pairs += [(x_ref, copies_ref.at[k]) for k in range(count)]
    moves = [
        pltpu.make_async_copy(source, target, sem.at[k])
        for k, (source, target) in enumerate(pairs)
    ]
    for move in moves[:4]:
        move.start()
    moves[0].wait()
    for move in moves[4:]:
        move.start()
    for move in moves[1:4]:
        move.wait()
    y = y_ref[...].astype(jnp.float32)
    bias = potential_ref[...] * 2.0 + logw_ref[...] - jnp.sum(y * y, axis=0, keepdims=True)
    out_ref[0:FEATURES, :] = (y * 2.0).astype(jnp.bfloat16)
    out_ref[FEATURES : FEATURES + EXTRA, :] = extra_block(
        three_parts(bias), ones_of(bias.shape[1])
    ).astype(jnp.bfloat16)
    for move in moves[4:]:
        move.wait()


def weights_of(features, extra):
    rest = jnp.zeros((DEPTH - FEATURES - EXTRA, features.shape[1]), features.dtype)
    return jnp.concatenate([features, extra, rest], axis=0)


def product(a, b):
    return jnp.dot(a, b, preferred_element_type=jnp.float32)


def folded(value, combine):
    rows, n = value.shape
    return combine(value.reshape(rows // 8, 8, n), axis=0)


def join(a, b):
    top = jnp.maximum(a, b)
    return top + jnp.log(1.0 + jnp.exp(jnp.minimum(a, b) - top))


def turn_kernel(y_ref, yt_ref):
    rows = yt_ref.shape[0]
    row_step = min(ROWS, rows)
    for k in range(0, rows, row_step):
        block = jnp.concatenate(
            [
                y_ref[:, k : k + row_step].astype(jnp.float32),
                jnp.zeros((DEPTH - FEATURES - EXTRA, row_step), jnp.float32),
            ],
            axis=0,
        )
        yt_ref[k : k + row_step, :] = block.T.astype(jnp.bfloat16)


def first_kernel(last, *refs):
    y_ref, x_ref, refs = refs[0], refs[1], refs[2:]
    if last:
        before_ref, logw_ref, yt_ref, l_ref, sums_ref = refs
        turn_kernel(y_ref, yt_ref)
    else:
        yt_ref, l_ref, sums_ref = refs
    rows = yt_ref.shape[0]
    ny, _, per = x_ref.shape
    row_step = min(ROWS, rows)
    col_step = min(LANES, per)
    together = 2

    extra = y_ref[FEATURES : FEATURES + EXTRA, :].astype(jnp.float32)
    bias = extra[0:1, :] + extra[1:2, :] + extra[2:3, :]
    shift = jnp.max(bias, axis=1, keepdims=True)
    extra = extra_block(
        ones_of(col_step), three_parts(jnp.broadcast_to(-shift, (1, col_step)))
    ).astype(jnp.bfloat16)

    def store(row, value):
        if last:
            value = join(before_ref[row : row + 1, :], value)
        l_ref[row : row + 1, 0:per] = value

    if last:
        part = per // ny
        for k in range(ny):
            l_ref[k : k + 1, per:] = logw_ref[:, k * part : (k + 1) * part]

    def main(g, carry):
        for s in range(together):
            r = g * together + s
            for t in range(0, per, col_step):
                weights = weights_of(x_ref[r, :, t : t + col_step], extra)
                total = jnp.zeros((8, col_step), jnp.float32)
                for j in range(0, rows, row_step):
                    score = product(yt_ref[j : j + row_step, :], weights)
                    total = total + folded(jnp.exp(score), jnp.sum)
                sums_ref[r, :, t : t + col_step] = total
        return carry

    lax.fori_loop(0, ny // together, main, 0)
    total = jnp.sum(sums_ref[...], axis=1)
    result = shift + jnp.log(total)
    for r in range(ny):
        store(r, result[r : r + 1, :])

    @pl.when(jnp.logical_not((jnp.min(total) > LOW) & (jnp.max(total) < HIGH)))
    def _():
        def again(g, carry):
            at = pl.ds(pl.multiple_of(g * col_step, col_step), col_step)
            for r in range(ny):
                weights = weights_of(x_ref[r, :, at], extra)

                def advance(j, state):
                    top, total = state
                    here = pl.ds(pl.multiple_of(j * row_step, row_step), row_step)
                    score = product(yt_ref[here, :], weights)
                    new = jnp.maximum(top, jnp.max(score, axis=0, keepdims=True))
                    total = total * jnp.exp(top - new) + jnp.sum(
                        jnp.exp(score - new), axis=0, keepdims=True
                    )
                    return new, total

                start = (
                    jnp.full((1, col_step), -1e30, jnp.float32),
                    jnp.zeros((1, col_step), jnp.float32),
                )
                top, total = lax.fori_loop(0, rows // row_step, advance, start)
                sums_ref[r, 0:1, at] = shift + top + jnp.log(total)
            return carry

        lax.fori_loop(0, per // col_step, again, 0)
        for r in range(ny):
            store(r, sums_ref[r, 0:1, :])


def second_kernel(
    slots,
    place_ref,
    near_ref,
    far_ref,
    x_ref,
    total_ref,
    logw_ref,
    s_ref,
    extra_ref,
    left_ref,
    acc_ref,
    top_ref,
):
    nz, each = s_ref.shape
    rows = nz * each
    ny, _, per = x_ref.shape
    row_step = min(ROWS, rows)
    col_step = min(LANES, per)

    for r in range(ny):
        logw = jnp.concatenate([logw_ref[r, k : k + 1, per:] for k in range(ny)], axis=1)
        c = logw - total_ref[r : r + 1, :]
        extra_ref[r] = extra_block(ones_of(per), three_parts(c)).astype(jnp.bfloat16)
    for g, (half, k, _) in enumerate(slots):
        ref = far_ref if half else near_ref
        left_ref[g * each : (g + 1) * each, :] = ref[k * each : (k + 1) * each, :]

    def lanes_folded(value, combine):
        out = value[:, 0:128]
        for k in range(1, value.shape[1] // 128):
            out = combine(out, value[:, k * 128 : (k + 1) * 128])
        return out

    def main(g, carry):
        here = pl.ds(pl.multiple_of(g * row_step, row_step), row_step)
        left = left_ref[here, :]
        for r in range(ny):
            for t in range(0, per, col_step):
                at = slice(t, t + col_step)
                score = product(left, weights_of(x_ref[r, :, at], extra_ref[r, :, at]))
                part = lanes_folded(jnp.exp(score), jnp.add)
                if r == 0 and t == 0:
                    acc_ref[here, :] = part
                else:
                    acc_ref[here, :] = acc_ref[here, :] + part
        return carry

    lax.fori_loop(0, rows // row_step, main, 0)

    def store(result):
        for g, (_, _, row) in enumerate(slots):
            s_ref[pl.ds(place_ref[0] ^ row, 1), :] = result[:, g * each : (g + 1) * each]

    total = jnp.sum(acc_ref[...].T, axis=0, keepdims=True)
    store(jnp.log(total))

    @pl.when(jnp.logical_not((jnp.min(total) > LOW) & (jnp.max(total) < HIGH)))
    def _():
        def again(g, carry):
            here = pl.ds(pl.multiple_of(g * each, each), each)
            left = left_ref[here, :]
            state = (
                jnp.full((each, 128), -1e30, jnp.float32),
                jnp.zeros((each, 128), jnp.float32),
            )
            for r in range(ny):

                def advance(t, state):
                    top, total = state
                    at = pl.ds(pl.multiple_of(t * col_step, col_step), col_step)
                    score = product(left, weights_of(x_ref[r, :, at], extra_ref[r, :, at]))
                    new = jnp.maximum(top, lanes_folded(score, jnp.maximum))
                    total = total * jnp.exp(top - new)
                    for k in range(col_step // 128):
                        total = total + jnp.exp(score[:, k * 128 : (k + 1) * 128] - new)
                    return new, total

                state = lax.fori_loop(0, per // col_step, advance, state)
            top_ref[here, :] = state[0]
            acc_ref[here, :] = state[1]
            return carry

        lax.fori_loop(0, rows // each, again, 0)
        tops = top_ref[...].T
        top = jnp.max(tops, axis=0, keepdims=True)
        total = jnp.sum(acc_ref[...].T * jnp.exp(tops - top), axis=0, keepdims=True)
        store(top + jnp.log(total))


def call(
    kernel, outs, scratch, flops, exps, *args, spaces=None, out=None, limit=40, moved=4 * 2**20
):
    out = out or jax.tree.map(lambda _: pltpu.VMEM, outs)
    return pl.pallas_call(
        kernel,
        out_shape=outs,
        in_specs=[
            pl.BlockSpec(memory_space=space) for space in spaces or [pltpu.VMEM] * len(args)
        ],
        out_specs=jax.tree.map(lambda space: pl.BlockSpec(memory_space=space), out),
        scratch_shapes=scratch,
        compiler_params=pltpu.CompilerParams(vmem_limit_bytes=limit * 2**20),
        cost_estimate=pl.CostEstimate(
            flops=flops, bytes_accessed=moved, transcendentals=exps
        ),
    )(*args)


def log_sum(parts):
    top = jnp.max(parts, axis=0)
    return top + jnp.log(jnp.sum(jnp.exp(parts - top), axis=0))


def per_device(nz, ny, nw, source_latent, source_logw, target_latent, target_logw, target_potential):
    f32, bf16 = jnp.float32, jnp.bfloat16
    per = source_latent.shape[0]
    each = target_latent.shape[0]
    cols, half = ny * per, nz // 2 * each
    pairs = cols * half
    place = lax.axis_index("blk")
    my_y, my_z = place // nz, place % nz
    depth = FEATURES + EXTRA
    y_groups = [[y * nz + z for y in range(ny)] for z in range(nz)]
    quarters = [[g * (nz // 2) + z for z in range(nz // 2)] for g in range(2 * ny)]
    x_groups = [[h * (nw // 2) + k for k in range(nw // 2)] for h in range(2)]

    def along_z(value, k):
        perm = [(y * nz + z, y * nz + (z ^ k)) for y in range(ny) for z in range(nz)]
        return lax.ppermute(value, "blk", perm)

    def along_wide(value, k):
        return lax.ppermute(value, "wide", [(w, w ^ k) for w in range(nw)])

    def shared(value, axis, groups):
        spread = jnp.broadcast_to(value[None], (len(groups[0]),) + value.shape)
        return lax.all_to_all(spread, axis, 0, 0, axis_index_groups=groups, tiled=True)

    x = source_latent.T
    y, copies = call(
        prepare_kernel,
        (
            jax.ShapeDtypeStruct((depth, each), bf16),
            jax.ShapeDtypeStruct((ny, FEATURES, per), bf16),
        ),
        [
            pltpu.VMEM((FEATURES, per), bf16),
            pltpu.VMEM((FEATURES, each), bf16),
            pltpu.VMEM((1, each), f32),
            pltpu.VMEM((1, each), f32),
            pltpu.SemaphoreType.DMA((4 + ny,)),
        ],
        each * FEATURES * 4,
        0,
        x,
        target_latent.T,
        target_logw.reshape(1, each),
        target_potential.reshape(1, each),
        spaces=[pl.ANY] * 4,
        out=(pltpu.VMEM, pl.ANY),
        limit=60,
    )
    xs = lax.all_to_all(copies, "blk", 0, 0, axis_index_groups=y_groups, tiled=True)
    bit = nz // 2
    while bit > 1:
        y = jnp.concatenate([y, along_z(y, bit)], axis=1)
        bit //= 2
    far = along_z(y, 1)

    def first(block, *more):
        last = len(more) == 2
        return call(
            functools.partial(first_kernel, last),
            (
                jax.ShapeDtypeStruct((half, DEPTH), bf16),
                jax.ShapeDtypeStruct((ny, per + per // ny), f32),
            )
            if last
            else jax.ShapeDtypeStruct((ny, per), f32),
            [pltpu.VMEM((ny, 8, per), f32)],
            2 * pairs * DEPTH,
            pairs,
            block,
            xs,
            *more,
        )

    yt_near = call(
        turn_kernel,
        jax.ShapeDtypeStruct((half, DEPTH), bf16),
        [],
        0,
        0,
        y,
        moved=60 * 10**6,
    )
    total = first(y, yt_near)
    yt_far, total = first(far, total, source_logw.reshape(1, per))
    got = shared(total, "blk", y_groups)
    total = log_sum(got[:, :, :per])
    total = log_sum(shared(total, "wide", x_groups))
    potential, mine, total = lax.optimization_barrier((target_potential, x, total))
    offset = lax.optimization_barrier(potential * 2.0 + target_logw)
    sq = lax.optimization_barrier(jnp.sum(jnp.square(mine.astype(f32)), axis=0, keepdims=True))
    total = join(total, along_wide(total, nw // 2))
    mine = lax.dynamic_slice(total, (my_y, 0), (1, per))
    source_potential = -0.5 * (mine - sq)

    count = nz // 2
    width = count.bit_length() - 1
    blocks = []
    for h in range(2):
        for k in range(count):
            blocks.append((h, k, 2 * int(format(k, "b").zfill(width)[::-1], 2) + h))
    place_in = (my_z % count).astype(jnp.int32).reshape(1)

    def second(slots, near):
        return call(
            functools.partial(second_kernel, slots),
            jax.ShapeDtypeStruct((count, each), f32),
            [
                pltpu.VMEM((ny, EXTRA, per), bf16),
                pltpu.VMEM((half, DEPTH), bf16),
                pltpu.VMEM((half, 128), f32),
                pltpu.VMEM((half, 128), f32),
            ],
            2 * pairs * DEPTH,
            pairs,
            place_in,
            near,
            yt_far,
            xs,
            total,
            got,
            spaces=[pltpu.SMEM] + [pltpu.VMEM] * 5,
        )

    sent = second(tuple((h, k, a - count) for h, k, a in blocks if a >= count), yt_near)
    yt_near, sent = lax.optimization_barrier((yt_near, sent))
    arrived = along_z(sent, count)
    sums = join(second(tuple(b for b in blocks if b[2] < count), yt_near), arrived)
    sums = lax.all_to_all(sums, "blk", 0, 0, axis_index_groups=quarters, tiled=True)
    new_target_potential = -0.5 * (log_sum(sums) - offset)
    return source_potential.reshape(per), new_target_potential


def solution(mesh):
    nz = ZRUN
    ny = mesh.shape["blk"] // nz
    nw = mesh.shape["wide"]
    placed = (
        P("blk", None),
        P("blk"),
        P(("wide", "blk"), None),
        P(("wide", "blk")),
        P(("wide", "blk")),
    )
    return jax.shard_map(
        functools.partial(per_device, nz, ny, nw),
        mesh=mesh,
        in_specs=placed,
        out_specs=(P("blk"), P(("wide", "blk"))),
        check_vma=False,
    )
```

```python
import functools

import jax
import jax.numpy as jnp
from jax import lax
from jax.experimental import pallas as pl
from jax.experimental.pallas import tpu as pltpu
from jax.sharding import PartitionSpec as P

ZRUN = 8
FEATURES = 64
EXTRA = 16
DEPTH = 128
ROWS = 512
LANES = 256
LOW = 2.0**-60
HIGH = 2.0**120


def three_parts(value):
    high = value.astype(jnp.bfloat16).astype(jnp.float32)
    rest = value - high
    middle = rest.astype(jnp.bfloat16).astype(jnp.float32)
    low = (rest - middle).astype(jnp.bfloat16).astype(jnp.float32)
    return high, middle, low


def extra_block(first, second):
    n = first[0].shape[1]
    row = lax.broadcasted_iota(jnp.int32, (EXTRA, n), 0)
    block = jnp.zeros((EXTRA, n), jnp.float32)
    for k, part in enumerate(tuple(first) + tuple(second)):
        block = jnp.where(row == k, part, block)
    return block


def ones_of(n):
    one = jnp.ones((1, n), jnp.float32)
    return one, one, one


def prepare_kernel(
    x_in, y_in, logw_in, potential_in, out_ref, offset_ref, copies_ref, x_ref, y_ref, logw_ref, potential_ref, sem
):
    count = copies_ref.shape[0]
    pairs = [(x_in, x_ref), (y_in, y_ref), (logw_in, logw_ref), (potential_in, potential_ref)]
    pairs += [(x_ref, copies_ref.at[k]) for k in range(count)]
    moves = [
        pltpu.make_async_copy(source, target, sem.at[k])
        for k, (source, target) in enumerate(pairs)
    ]
    for move in moves[:4]:
        move.start()
    moves[0].wait()
    for move in moves[4:]:
        move.start()
    for move in moves[1:4]:
        move.wait()
    y = y_ref[...].astype(jnp.float32)
    offset = potential_ref[...] * 2.0 + logw_ref[...]
    bias = offset - jnp.sum(y * y, axis=0, keepdims=True)
    out_ref[0:FEATURES, :] = (y * 2.0).astype(jnp.bfloat16)
    out_ref[FEATURES : FEATURES + EXTRA, :] = extra_block(
        three_parts(bias), ones_of(bias.shape[1])
    ).astype(jnp.bfloat16)
    offset_ref[...] = offset
    for move in moves[4:]:
        move.wait()


def weights_of(features, extra):
    rest = jnp.zeros((DEPTH - FEATURES - EXTRA, features.shape[1]), features.dtype)
    return jnp.concatenate([features, extra, rest], axis=0)


def product(a, b):
    return jnp.dot(a, b, preferred_element_type=jnp.float32)


def folded(value, combine):
    rows, n = value.shape
    return combine(value.reshape(rows // 8, 8, n), axis=0)


def join(a, b):
    top = jnp.maximum(a, b)
    return top + jnp.log(1.0 + jnp.exp(jnp.minimum(a, b) - top))


def turn_kernel(y_ref, yt_ref):
    rows = yt_ref.shape[0]
    row_step = min(ROWS, rows)
    for k in range(0, rows, row_step):
        block = jnp.concatenate(
            [
                y_ref[:, k : k + row_step].astype(jnp.float32),
                jnp.zeros((DEPTH - FEATURES - EXTRA, row_step), jnp.float32),
            ],
            axis=0,
        )
        yt_ref[k : k + row_step, :] = block.T.astype(jnp.bfloat16)


def first_kernel(last, *refs):
    y_ref, x_ref, refs = refs[0], refs[1], refs[2:]
    if last:
        before_ref, logw_ref, offset_ref, yt_ref, l_ref, kept_ref, sums_ref = refs
        turn_kernel(y_ref, yt_ref)
        kept_ref[...] = offset_ref[...]
    else:
        yt_ref, l_ref, sums_ref = refs
    rows = yt_ref.shape[0]
    ny, _, per = x_ref.shape
    row_step = min(ROWS, rows)
    col_step = min(LANES, per)
    together = 2

    extra = y_ref[FEATURES : FEATURES + EXTRA, :].astype(jnp.float32)
    bias = extra[0:1, :] + extra[1:2, :] + extra[2:3, :]
    shift = jnp.max(bias, axis=1, keepdims=True)
    extra = extra_block(
        ones_of(col_step), three_parts(jnp.broadcast_to(-shift, (1, col_step)))
    ).astype(jnp.bfloat16)

    def store(row, value):
        if last:
            value = join(before_ref[row : row + 1, :], value)
        l_ref[row : row + 1, 0:per] = value

    if last:
        part = per // ny
        for k in range(ny):
            l_ref[k : k + 1, per:] = logw_ref[:, k * part : (k + 1) * part]

    def main(g, carry):
        for s in range(together):
            r = g * together + s
            for t in range(0, per, col_step):
                weights = weights_of(x_ref[r, :, t : t + col_step], extra)
                total = jnp.zeros((8, col_step), jnp.float32)
                for j in range(0, rows, row_step):
                    score = product(yt_ref[j : j + row_step, :], weights)
                    total = total + folded(jnp.exp(score), jnp.sum)
                sums_ref[r, :, t : t + col_step] = total
        return carry

    lax.fori_loop(0, ny // together, main, 0)
    total = jnp.sum(sums_ref[...], axis=1)
    result = shift + jnp.log(total)
    for r in range(ny):
        store(r, result[r : r + 1, :])

    @pl.when(jnp.logical_not((jnp.min(total) > LOW) & (jnp.max(total) < HIGH)))
    def _():
        def again(g, carry):
            at = pl.ds(pl.multiple_of(g * col_step, col_step), col_step)
            for r in range(ny):
                weights = weights_of(x_ref[r, :, at], extra)

                def advance(j, state):
                    top, total = state
                    here = pl.ds(pl.multiple_of(j * row_step, row_step), row_step)
                    score = product(yt_ref[here, :], weights)
                    new = jnp.maximum(top, jnp.max(score, axis=0, keepdims=True))
                    total = total * jnp.exp(top - new) + jnp.sum(
                        jnp.exp(score - new), axis=0, keepdims=True
                    )
                    return new, total

                start = (
                    jnp.full((1, col_step), -1e30, jnp.float32),
                    jnp.zeros((1, col_step), jnp.float32),
                )
                top, total = lax.fori_loop(0, rows // row_step, advance, start)
                sums_ref[r, 0:1, at] = shift + top + jnp.log(total)
            return carry

        lax.fori_loop(0, per // col_step, again, 0)
        for r in range(ny):
            store(r, sums_ref[r, 0:1, :])


def second_kernel(
    slots,
    place_ref,
    near_ref,
    far_ref,
    x_ref,
    total_ref,
    logw_ref,
    s_ref,
    extra_ref,
    left_ref,
    acc_ref,
    top_ref,
):
    nz, each = s_ref.shape
    rows = nz * each
    ny, _, per = x_ref.shape
    row_step = min(ROWS, rows)
    col_step = min(LANES, per)

    for r in range(ny):
        logw = jnp.concatenate([logw_ref[r, k : k + 1, per:] for k in range(ny)], axis=1)
        c = logw - total_ref[r : r + 1, :]
        extra_ref[r] = extra_block(ones_of(per), three_parts(c)).astype(jnp.bfloat16)
    for g, (half, k, _) in enumerate(slots):
        ref = far_ref if half else near_ref
        left_ref[g * each : (g + 1) * each, :] = ref[k * each : (k + 1) * each, :]

    def lanes_folded(value, combine):
        out = value[:, 0:128]
        for k in range(1, value.shape[1] // 128):
            out = combine(out, value[:, k * 128 : (k + 1) * 128])
        return out

    def main(g, carry):
        here = pl.ds(pl.multiple_of(g * row_step, row_step), row_step)
        left = left_ref[here, :]
        for r in range(ny):
            for t in range(0, per, col_step):
                at = slice(t, t + col_step)
                score = product(left, weights_of(x_ref[r, :, at], extra_ref[r, :, at]))
                part = lanes_folded(jnp.exp(score), jnp.add)
                if r == 0 and t == 0:
                    acc_ref[here, :] = part
                else:
                    acc_ref[here, :] = acc_ref[here, :] + part
        return carry

    lax.fori_loop(0, rows // row_step, main, 0)

    def store(result):
        for g, (_, _, row) in enumerate(slots):
            s_ref[pl.ds(place_ref[0] ^ row, 1), :] = result[:, g * each : (g + 1) * each]

    total = jnp.sum(acc_ref[...].T, axis=0, keepdims=True)
    store(jnp.log(total))

    @pl.when(jnp.logical_not((jnp.min(total) > LOW) & (jnp.max(total) < HIGH)))
    def _():
        def again(g, carry):
            here = pl.ds(pl.multiple_of(g * each, each), each)
            left = left_ref[here, :]
            state = (
                jnp.full((each, 128), -1e30, jnp.float32),
                jnp.zeros((each, 128), jnp.float32),
            )
            for r in range(ny):

                def advance(t, state):
                    top, total = state
                    at = pl.ds(pl.multiple_of(t * col_step, col_step), col_step)
                    score = product(left, weights_of(x_ref[r, :, at], extra_ref[r, :, at]))
                    new = jnp.maximum(top, lanes_folded(score, jnp.maximum))
                    total = total * jnp.exp(top - new)
                    for k in range(col_step // 128):
                        total = total + jnp.exp(score[:, k * 128 : (k + 1) * 128] - new)
                    return new, total

                state = lax.fori_loop(0, per // col_step, advance, state)
            top_ref[here, :] = state[0]
            acc_ref[here, :] = state[1]
            return carry

        lax.fori_loop(0, rows // each, again, 0)
        tops = top_ref[...].T
        top = jnp.max(tops, axis=0, keepdims=True)
        total = jnp.sum(acc_ref[...].T * jnp.exp(tops - top), axis=0, keepdims=True)
        store(top + jnp.log(total))


def call(kernel, outs, scratch, flops, exps, *args, spaces=None, out=None, limit=40):
    out = out or jax.tree.map(lambda _: pltpu.VMEM, outs)
    return pl.pallas_call(
        kernel,
        out_shape=outs,
        in_specs=[
            pl.BlockSpec(memory_space=space) for space in spaces or [pltpu.VMEM] * len(args)
        ],
        out_specs=jax.tree.map(lambda space: pl.BlockSpec(memory_space=space), out),
        scratch_shapes=scratch,
        compiler_params=pltpu.CompilerParams(vmem_limit_bytes=limit * 2**20),
        cost_estimate=pl.CostEstimate(
            flops=flops, bytes_accessed=4 * 2**20, transcendentals=exps
        ),
    )(*args)


def log_sum(parts):
    top = jnp.max(parts, axis=0)
    return top + jnp.log(jnp.sum(jnp.exp(parts - top), axis=0))


def per_device(nz, ny, nw, source_latent, source_logw, target_latent, target_logw, target_potential):
    f32, bf16 = jnp.float32, jnp.bfloat16
    per = source_latent.shape[0]
    each = target_latent.shape[0]
    cols, half = ny * per, nz // 2 * each
    pairs = cols * half
    place = lax.axis_index("blk")
    my_y, my_z = place // nz, place % nz
    depth = FEATURES + EXTRA
    y_groups = [[y * nz + z for y in range(ny)] for z in range(nz)]
    quarters = [[g * (nz // 2) + z for z in range(nz // 2)] for g in range(2 * ny)]
    x_groups = [[h * (nw // 2) + k for k in range(nw // 2)] for h in range(2)]

    def along_z(value, k):
        perm = [(y * nz + z, y * nz + (z ^ k)) for y in range(ny) for z in range(nz)]
        return lax.ppermute(value, "blk", perm)

    def along_wide(value, k):
        return lax.ppermute(value, "wide", [(w, w ^ k) for w in range(nw)])

    def shared(value, axis, groups):
        spread = jnp.broadcast_to(value[None], (len(groups[0]),) + value.shape)
        return lax.all_to_all(spread, axis, 0, 0, axis_index_groups=groups, tiled=True)

    x = source_latent.T
    y, offset, copies = call(
        prepare_kernel,
        (
            jax.ShapeDtypeStruct((depth, each), bf16),
            jax.ShapeDtypeStruct((1, each), f32),
            jax.ShapeDtypeStruct((ny, FEATURES, per), bf16),
        ),
        [
            pltpu.VMEM((FEATURES, per), bf16),
            pltpu.VMEM((FEATURES, each), bf16),
            pltpu.VMEM((1, each), f32),
            pltpu.VMEM((1, each), f32),
            pltpu.SemaphoreType.DMA((4 + ny,)),
        ],
        each * FEATURES * 4,
        0,
        x,
        target_latent.T,
        target_logw.reshape(1, each),
        target_potential.reshape(1, each),
        spaces=[pl.ANY] * 4,
        out=(pltpu.VMEM, pltpu.VMEM, pl.ANY),
        limit=60,
    )
    xs = lax.all_to_all(copies, "blk", 0, 0, axis_index_groups=y_groups, tiled=True)
    bit = nz // 2
    while bit > 1:
        y = jnp.concatenate([y, along_z(y, bit)], axis=1)
        bit //= 2
    far = along_z(y, 1)

    def first(block, *more):
        last = len(more) == 3
        return call(
            functools.partial(first_kernel, last),
            (
                jax.ShapeDtypeStruct((half, DEPTH), bf16),
                jax.ShapeDtypeStruct((ny, per + per // ny), f32),
                jax.ShapeDtypeStruct((1, each), f32),
            )
            if last
            else jax.ShapeDtypeStruct((ny, per), f32),
            [pltpu.VMEM((ny, 8, per), f32)],
            2 * pairs * DEPTH,
            pairs,
            block,
            xs,
            *more,
        )

    yt_near = call(
        turn_kernel,
        jax.ShapeDtypeStruct((half, DEPTH), bf16),
        [],
        0,
        0,
        y,
    )
    total = first(y, yt_near)
    yt_far, total, offset = first(far, total, source_logw.reshape(1, per), offset)
    got = shared(total, "blk", y_groups)
    total = log_sum(got[:, :, :per])
    total = log_sum(shared(total, "wide", x_groups))
    total = join(total, along_wide(total, nw // 2))
    sq = jnp.sum(jnp.square(x.astype(f32)), axis=0, keepdims=True)
    mine = lax.dynamic_slice(total, (my_y, 0), (1, per))
    source_potential = -0.5 * (mine - sq)

    count = nz // 2
    width = count.bit_length() - 1
    blocks = []
    for h in range(2):
        for k in range(count):
            blocks.append((h, k, 2 * int(format(k, "b").zfill(width)[::-1], 2) + h))
    place_in = (my_z % count).astype(jnp.int32).reshape(1)

    def second(slots, near):
        return call(
            functools.partial(second_kernel, slots),
            jax.ShapeDtypeStruct((count, each), f32),
            [
                pltpu.VMEM((ny, EXTRA, per), bf16),
                pltpu.VMEM((half, DEPTH), bf16),
                pltpu.VMEM((half, 128), f32),
                pltpu.VMEM((half, 128), f32),
            ],
            2 * pairs * DEPTH,
            pairs,
            place_in,
            near,
            yt_far,
            xs,
            total,
            got,
            spaces=[pltpu.SMEM] + [pltpu.VMEM] * 5,
        )

    sent = second(tuple((h, k, a - count) for h, k, a in blocks if a >= count), yt_near)
    yt_near, sent = lax.optimization_barrier((yt_near, sent))
    arrived = along_z(sent, count)
    sums = join(second(tuple(b for b in blocks if b[2] < count), yt_near), arrived)
    sums = lax.all_to_all(sums, "blk", 0, 0, axis_index_groups=quarters, tiled=True)
    new_target_potential = -0.5 * (log_sum(sums) - offset[0])
    return source_potential.reshape(per), new_target_potential


def solution(mesh):
    nz = ZRUN
    ny = mesh.shape["blk"] // nz
    nw = mesh.shape["wide"]
    placed = (
        P("blk", None),
        P("blk"),
        P(("wide", "blk"), None),
        P(("wide", "blk")),
        P(("wide", "blk")),
    )
    return jax.shard_map(
        functools.partial(per_device, nz, ny, nw),
        mesh=mesh,
        in_specs=placed,
        out_specs=(P("blk"), P(("wide", "blk"))),
        check_vma=False,
    )
```
